32 devices in a mesh: groups: 2 (over y), locus: 4 (over z), design: 2 (over x), chan: 2 (over core).
Axes of the slice: x: 2, y: 2, z: 4, core: 2. Of those that a mesh axis runs over, the one named last changes fastest.
Arguments:
- base_seq: bfloat16 [4, 2048, 128], P(('groups', 'design'), 'locus'), parts along dimension 0, may hold values from -6 to 6
- deltas: bfloat16 [2048, 512], P(('groups', 'locus', 'design')), parts along dimension 0, may hold values from -6 to 6
- owners: int32 [2048, 1], P(('groups', 'locus', 'design')), parts along dimension 0, may hold values from 0 to 7; in each aligned block of 128 rows (0 to 127, 128 to 255, ...) at most 32 rows name the same one
- slot_ids: int32 [2048], P(('groups', 'locus', 'design')), parts along dimension 0, may hold values from 0 to 127
- stem_weight: bfloat16 [128, 1536], P(None, 'chan'), may hold values from -0.5 to 0.5
- dilated_tap_weight: bfloat16 [3, 1536, 768], P(None, None, 'chan'), may hold values from -0.09375 to 0.09375
- mix_weight: bfloat16 [768, 1536], P('chan'), may hold values from -0.21875 to 0.21875
- head_weight: bfloat16 [1536], replicated, may hold values from -5 to 5
Outputs:
- window_grad: float32 [2048, 512], P(('groups', 'locus', 'design')), parts along dimension 0
The draws below stay inside these ranges and needn't reach their ends.
There are 2 independent parts, one for each index of `groups`. The reference program is written for one: setup_inputs(seed, part) draws one part's arguments, and reference() takes and returns one part's arrays. A program takes and returns all parts, laid end to end along the dimension named above; an argument that names none is the same for every part. Nothing has to cross between parts.
Inputs may be any that keep to these rules, and one draw needn't show every extreme that they name: `owners`: owner o stands for bins of segment o // 2 of locus o % 2. Among the 128 windows of one device no owner is named more than 32 times, a bound that some block reaches. `slot_ids`: several windows may name the same target; their changes add.
All inputs are finite; a program needn't handle non-finite values.
Results may differ from the reference program's by a relative error of at most 0.0055.
Values may be sent and summed in bfloat16 or wider, within the bound.
A program may use at most 64 MiB of HBM per device.

```python
import math
import jax
import jax.numpy as jnp
import numpy as np
from jax import lax

C = 1536
F = 128
WIN_BINS = 4
DILATION_STEP = 32
WIN_DEV = 128
CAP = 32
NBINS = 2048
SLOTS_DEV = 128
LOCI = 2
WINDOWS = 1024
N_LOCUS = 4
N_DESIGN = 2


def set_ends(drawn, own_key, low, largest):
    longest = drawn.shape.index(max(drawn.shape))
    spots = []
    for shift in (0, 1):
        where = [jax.random.randint(jax.random.fold_in(own_key, axis), (), 0, length) for axis, length in enumerate(drawn.shape)]
        where[longest] = (where[longest] + shift) % drawn.shape[longest]
        spots.append(tuple(where))
    return drawn.at[spots[0]].set(low).at[spots[1]].set(largest)


def block_levels(stream_key, shape, shards, low, largest):
    def one(dim, parts):
        draws = jax.random.uniform(jax.random.fold_in(jax.random.fold_in(stream_key, 6), dim), (parts,), jnp.float32, low / len(shards), largest / len(shards))
        return jnp.repeat(jnp.exp(draws), shape[dim] // parts).reshape((-1,) + (1,) * (len(shape) - dim - 1))

    factor_of = one(*shards[0])
    for cut in shards[1:]:
        factor_of = factor_of * one(*cut)
    return factor_of


def shared_out(rng, own, number, rows, number_of, top, most, lean):
    order = jax.random.permutation(rng, number_of)
    crowded, common = portions_of(number_of, rows * top, most, lean, True), portions_of(number_of, rows * top, most, lean, False)
    places = jnp.arange(number_of)

    def named(sizes, rotation):
        used = int((sizes > 0).sum())
        fixed = max(1, used // 4)
        moved = fixed + (places - fixed + rotation * (used - fixed)) % max(1, number_of - fixed)
        return jnp.zeros((number_of,), jnp.int32).at[order[jnp.where(places < fixed, places, moved)]].set(jnp.asarray(sizes, jnp.int32))

    sizes = jnp.where(number % 4 == 0, named(crowded, number // 4), named(common, number - number // 4 - 1))
    mixed = jax.random.permutation(jax.random.fold_in(own, 3), number_of)
    donor, taker = mixed[0:number_of // 2 * 2:2], mixed[1:number_of // 2 * 2:2]
    slack = jnp.minimum(sizes[donor] - 1, most - sizes[taker]) // 2
    slack = jnp.where((donor == order[0]) | (taker == order[0]) | (sizes[taker] == 0), 0, jnp.maximum(slack, 0))
    moved = jax.random.randint(jax.random.fold_in(own, 4), (number_of // 2,), 0, 1 << 20) % (slack + 1)
    sizes = sizes.at[donor].add(-moved).at[taker].add(moved)
    labels = jnp.searchsorted(jnp.cumsum(sizes), jnp.arange(rows * top), side="right").astype(jnp.int32)
    listing = labels.reshape(top, rows).T
    listing = listing[jax.random.permutation(jax.random.fold_in(own, 1), rows)]
    rotation = jax.random.randint(jax.random.fold_in(own, 2), (rows, 1), 0, top)
    return jnp.take_along_axis(listing, (jnp.arange(top)[None, :] + rotation) % top, axis=1)


def portions_of(count, total, most, slope, full):
    weights = [(1 << 20) // math.isqrt(standing ** slope) + 1 for standing in range(1, count + 1)]
    largest = most if full else min(most, max(-(-total // count), total * weights[0] // sum(weights)))
    least = 1 if total - largest >= count - 1 else 0
    holding, surplus = [largest] + [least] * (count - 1), total - largest - least * (count - 1)
    while surplus > 0:
        free = [i for i in range(1, count) if holding[i] < largest] or [i for i in range(1, count) if holding[i] < most]
        pool, budget = sum([weights[i] for i in free]), surplus
        for i in free:
            addition = min(most - holding[i], max(1, budget * weights[i] // pool), surplus)
            holding[i] = holding[i] + addition
            surplus = surplus - addition
    return np.array(holding)


def scatter_about(rng, dims, deviation, most, split=(), dtype=jnp.bfloat16):
    level = block_levels(rng, dims, split, -0.22, 0.18) if split else 1.0
    drawn = jax.random.normal(rng, dims, jnp.float32) * deviation * level
    return jnp.minimum(jnp.maximum(drawn, -most), most).astype(dtype)


def setup_inputs(seed: int = 0, part: int = 0) -> dict:
    keys = jax.random.split(jax.random.key(seed), 9)
    own_keys = jax.random.split(jax.random.fold_in(keys[8], part), 9)
    base_seq = scatter_about(own_keys[0], (LOCI, NBINS, F), 1.0, 6.0, ((0, 2), (1, 4)))
    deltas = scatter_about(own_keys[1], (WINDOWS, WIN_BINS * F), 1.0, 6.0, ((0, 8),))
    owners_keys = jax.random.split(jax.random.fold_in(own_keys[2], 1), WINDOWS // WIN_DEV)
    owners_turns = jax.random.permutation(jax.random.fold_in(own_keys[2], 3), WINDOWS // WIN_DEV)
    owners = jax.vmap(lambda own, number: shared_out(jax.random.fold_in(own_keys[2], 2), own, number, WIN_DEV, N_LOCUS * N_DESIGN, 1, CAP, 2))(owners_keys, owners_turns).reshape((WINDOWS, 1))
    slot_ids = set_ends(jax.random.randint(own_keys[3], (WINDOWS,), 0, SLOTS_DEV), jax.random.fold_in(own_keys[3], 1), 0, SLOTS_DEV - 1).astype(jnp.int32)
    stem_weight = scatter_about(keys[4], (F, C), F ** -0.5, 0.5, ((1, 2),))
    dilated_tap_weight = scatter_about(keys[5], (3, C, C // 2), (3 * C) ** -0.5, 0.09375, ((2, 2),))
    mix_weight = scatter_about(keys[6], (C // 2, C), (C // 2) ** -0.5, 0.21875, ((0, 2),))
    head_weight = scatter_about(keys[7], (C,), 1.0, 5.0)
    return {"base_seq": base_seq, "deltas": deltas, "owners": owners, "slot_ids": slot_ids, "stem_weight": stem_weight, "dilated_tap_weight": dilated_tap_weight, "mix_weight": mix_weight, "head_weight": head_weight}


def silu_slope(pre_value):
    sigmoid_value = jax.nn.sigmoid(pre_value)
    return sigmoid_value * (1.0 + pre_value * (1.0 - sigmoid_value))

def gelu_pull(pre_act, cotangent):
    return jax.vjp(lambda argument: jax.nn.gelu(argument, approximate=True), pre_act)[1](cotangent)[0]

def reference(base_seq, deltas, owners, slot_ids, stem_weight, dilated_tap_weight, mix_weight, head_weight):
    locus_count, count_of_bins, feat_width = base_seq.shape
    row_width = deltas.shape[1]
    slots_all = count_of_bins * feat_width // row_width
    target_dev = owners[:, 0]
    target = (target_dev % N_DESIGN * slots_all + target_dev // N_DESIGN * SLOTS_DEV + slot_ids).astype(jnp.int32)
    edit_sum = jax.ops.segment_sum(deltas.astype(jnp.float32), target, num_segments=locus_count * slots_all)
    sequence_onehot = (base_seq.astype(jnp.float32) + edit_sum.reshape(locus_count, count_of_bins, feat_width)).astype(jnp.bfloat16)
    mix_grad = jnp.dot(mix_weight, head_weight, preferred_element_type=jnp.float32)
    head_wide = head_weight.astype(jnp.float32)
    stem_wide = stem_weight.astype(jnp.float32)

    def one_locus(seq_one):
        pre_act = jnp.dot(seq_one, stem_weight, preferred_element_type=jnp.float32)
        hidden_state = jax.nn.gelu(pre_act, approximate=True).astype(jnp.bfloat16)
        padded_input = jnp.pad(hidden_state, ((DILATION_STEP, DILATION_STEP), (0, 0)))
        convolved_output = jnp.zeros((count_of_bins, mix_grad.shape[0]), jnp.float32)
        for filter_tap in range(3):
            convolved_output = convolved_output + jnp.dot(padded_input[filter_tap * DILATION_STEP:filter_tap * DILATION_STEP + count_of_bins], dilated_tap_weight[filter_tap], preferred_element_type=jnp.float32)
        residual_branch = (silu_slope(convolved_output) * mix_grad[None, :]).astype(jnp.bfloat16)
        padded_gradient = jnp.pad(residual_branch, ((DILATION_STEP, DILATION_STEP), (0, 0)))
        hidden_grad = jnp.broadcast_to(head_wide[None, :], pre_act.shape)
        for filter_tap in range(3):
            lower_boundary = (2 - filter_tap) * DILATION_STEP
            hidden_grad = hidden_grad + jnp.dot(padded_gradient[lower_boundary:lower_boundary + count_of_bins], dilated_tap_weight[filter_tap].T, preferred_element_type=jnp.float32)
        pulled = gelu_pull(pre_act, hidden_grad)
        return jnp.dot(pulled, stem_wide.T, precision=lax.Precision.HIGHEST)
    seq_grad = lax.map(one_locus, sequence_onehot)
    return seq_grad.reshape(locus_count * slots_all, row_width)[target]
```

```python
import functools

import jax
import jax.numpy as jnp
from jax import lax
from jax.experimental import pallas as pl
from jax.experimental.pallas import tpu as pltpu
from jax.sharding import PartitionSpec as P

DILATION_STEP = 32
MESH = pl.DeviceIdType.MESH
NT = (((1,), (1,)), ((), ()))


def with_halo(cells, sides, width):
    for axis, dim in sides:
        count = lax.axis_size(axis)
        ends = count - 1
        head = lax.slice_in_dim(cells, 0, width, axis=dim)
        tail = lax.slice_in_dim(cells, cells.shape[dim] - width, cells.shape[dim], axis=dim)
        cells = jnp.concatenate(
            [
                lax.ppermute(tail, axis, [(i, (i + 1) % count) for i in range(ends)]),
                cells,
                lax.ppermute(head, axis, [((i + 1) % count, i) for i in range(ends)]),
            ],
            axis=dim,
        )
    return cells


def silu_slope(pre_value):
    sigmoid_value = jax.nn.sigmoid(pre_value)
    return sigmoid_value * (1.0 + pre_value * (1.0 - sigmoid_value))


def gelu_pull(pre_act, cotangent):
    return jax.vjp(lambda argument: jax.nn.gelu(argument, approximate=True), pre_act)[1](cotangent)[
        0
    ]


def stem_back(pulled, weight):
    upper = pulled.astype(jnp.bfloat16)
    lower = (pulled - upper.astype(jnp.float32)).astype(jnp.bfloat16)
    dims = (((1,), (1,)), ((), ()))
    first = lax.dot_general(upper, weight, dims, preferred_element_type=jnp.float32)
    return first + lax.dot_general(lower, weight, dims, preferred_element_type=jnp.float32)


def shards(
    base_seq, deltas, owners, slot_ids, stem_weight, dilated_tap_weight, mix_weight, head_weight
):
    win_dev, row_width = deltas.shape
    bins_per_device, feat_width = (base_seq.shape[1], base_seq.shape[2])
    slots_dev = bins_per_device * feat_width // row_width
    peer_count = lax.axis_size(("locus", "design"))
    capacity = max(2, 2 * win_dev // peer_count)
    bucket_rows = peer_count * capacity
    target_dev = owners[:, 0]
    member = (target_dev[:, None] == jnp.arange(peer_count, dtype=jnp.int32)[None, :]).astype(
        jnp.int32
    )
    order = jnp.arange(win_dev, dtype=jnp.int32)
    before = (order[None, :] < order[:, None]).astype(jnp.bfloat16)
    earlier = jnp.dot(
        before, member.astype(jnp.bfloat16), preferred_element_type=jnp.float32
    ).astype(jnp.int32)
    bucket_rank = jnp.sum(earlier * member, axis=1)
    position = target_dev * capacity + bucket_rank
    placer = position[None, :] == jnp.arange(bucket_rows, dtype=jnp.int32)[:, None]
    send_rows = jnp.dot(
        placer.astype(jnp.bfloat16), deltas, preferred_element_type=jnp.float32
    ).astype(jnp.bfloat16)
    send_slots = jnp.sum(jnp.where(placer, slot_ids[None, :], 0), axis=1)
    recv_rows, recv_slots = (
        lax.all_to_all(send_rows, ("locus", "design"), split_axis=0, concat_axis=0, tiled=True),
        lax.all_to_all(send_slots, ("locus", "design"), split_axis=0, concat_axis=0, tiled=True),
    )
    chooser = recv_slots[:, None] == jnp.arange(slots_dev, dtype=jnp.int32)[None, :]
    edit_sum = lax.dot_general(
        chooser.astype(jnp.bfloat16),
        recv_rows,
        (((0,), (0,)), ((), ())),
        preferred_element_type=jnp.float32,
    )
    sequence_onehot = (
        base_seq[0].astype(jnp.float32) + edit_sum.reshape(bins_per_device, feat_width)
    ).astype(jnp.bfloat16)
    padded_sequence = with_halo(sequence_onehot, (("locus", 0),), DILATION_STEP)
    stem_full = lax.all_gather(stem_weight, "chan", axis=1, tiled=True)
    gathered_preactivation = jnp.dot(padded_sequence, stem_full, preferred_element_type=jnp.float32)
    hidden_state = jax.nn.gelu(gathered_preactivation, approximate=True).astype(jnp.bfloat16)
    own_width = dilated_tap_weight.shape[2]
    convolved_output = jnp.zeros((bins_per_device, own_width), jnp.float32)
    for filter_tap in range(3):
        convolved_output = convolved_output + jnp.dot(
            hidden_state[filter_tap * DILATION_STEP : filter_tap * DILATION_STEP + bins_per_device],
            dilated_tap_weight[filter_tap],
            preferred_element_type=jnp.float32,
        )
    mix_grad = jnp.dot(mix_weight, head_weight, preferred_element_type=jnp.float32)
    residual_branch = (silu_slope(convolved_output) * mix_grad[None, :]).astype(jnp.bfloat16)
    padded_gradient = with_halo(residual_branch, (("locus", 0),), DILATION_STEP)
    part_sum = jnp.zeros((bins_per_device, stem_full.shape[1]), jnp.float32)
    for filter_tap in range(3):
        lower_boundary = (2 - filter_tap) * DILATION_STEP
        part_sum = part_sum + lax.dot_general(
            padded_gradient[lower_boundary : lower_boundary + bins_per_device],
            dilated_tap_weight[filter_tap],
            (((1,), (1,)), ((), ())),
            preferred_element_type=jnp.float32,
        )
    local_preactivation = gathered_preactivation[DILATION_STEP : DILATION_STEP + bins_per_device]
    summed = lax.psum(part_sum, "chan")
    hidden_grad = head_weight.astype(jnp.float32)[None, :] + summed
    pulled = gelu_pull(local_preactivation, hidden_grad)
    seq_grad = stem_back(pulled, stem_full)
    slot_grad = seq_grad.reshape(slots_dev, row_width)
    back_rows = jnp.dot(chooser.astype(jnp.float32), slot_grad, precision=lax.Precision.HIGHEST)
    returned = lax.all_to_all(
        back_rows, ("locus", "design"), split_axis=0, concat_axis=0, tiled=True
    )
    return lax.dot_general(
        placer.astype(jnp.float32),
        returned,
        (((0,), (0,)), ((), ())),
        precision=lax.Precision.HIGHEST,
    )


def dot(left, right):
    return jnp.dot(left, right, preferred_element_type=jnp.float32)


def dot_nt(left, right):
    return lax.dot_general(left, right, NT, preferred_element_type=jnp.float32)


def iota(shape, axis):
    return lax.broadcasted_iota(jnp.int32, shape, axis)


def to_column(row):
    count = row.shape[1]
    eye = iota((count, count), 0) == iota((count, count), 1)
    return jnp.sum(jnp.where(eye, row, 0.0), axis=1, keepdims=True)


def gelu_parts(value):
    square = value * value
    root = 0.7978845608028654
    curve = jnp.tanh(value * (root + (root * 0.044715) * square))
    return square, curve


def gelu_value(value):
    half = 0.5 * value
    return half + half * gelu_parts(value)[1]


def gelu_slope(value):
    square, curve = gelu_parts(value)
    root = 0.7978845608028654
    inner = value * (root + (3.0 * root * 0.044715) * square)
    return 0.5 * (1.0 + curve) + 0.5 * (1.0 - curve * curve) * inner


def kernel(
    n_locus,
    n_design,
    base_ref,
    deltas_ref,
    owners_ref,
    slots_ref,
    stem_hbm,
    taps_hbm,
    mix_hbm,
    head_ref,
    out_ref,
    stem_ref,
    taps_ref,
    mix_ref,
    send_rows,
    send_slots,
    recv_rows,
    recv_slots,
    seq_ref,
    hidden_ref,
    branch_ref,
    part_send,
    part_recv,
    back_ref,
    ret_ref,
    half_ref,
    other_ref,
    load_sem,
    rows_sem,
    slots_sem,
    stem_sem,
    seq_sem,
    halo_sem,
    part_sem,
    back_sem,
    half_sem,
):
    group, locus = lax.axis_index("groups"), lax.axis_index("locus")
    design, core = lax.axis_index("design"), lax.axis_index("chan")
    peers = n_locus * n_design
    me = locus * n_design + design
    wins, width = deltas_ref.shape
    half_width = width // 2
    cap = recv_rows.shape[1]
    stem_half = stem_hbm.shape[1]
    channels = stem_ref.shape[1]
    blocks = seq_ref.shape[0] - 4
    slots = blocks * 8
    tile = part_send.shape[2]
    tiles = channels // tile
    mates = 1 - core
    partner = (group, locus, design, mates)

    def peer(index):
        return (group, index // n_design, index % n_design, core)

    own_columns = pl.ds(pl.multiple_of(core * half_width, half_width), half_width)
    other_columns = pl.ds(pl.multiple_of(mates * half_width, half_width), half_width)
    own_stem = pl.ds(pl.multiple_of(core * stem_half, stem_half), stem_half)

    load_taps = pltpu.make_async_copy(taps_hbm, taps_ref, load_sem.at[0])
    load_mix = pltpu.make_async_copy(mix_hbm, mix_ref, load_sem.at[1])
    load_stem = pltpu.make_async_copy(stem_hbm, stem_ref.at[:, own_stem], load_sem.at[2])
    load_stem.start()
    load_mix.start()
    load_taps.start()

    barrier = pltpu.get_barrier_semaphore()

    def greet(device):
        pl.semaphore_signal(barrier, inc=1, device_id=device, device_id_type=MESH)

    for step in range(1, peers):
        greet(peer((me + step) % peers))
    greet(partner)

    @pl.when(locus > 0)
    def _():
        greet((group, locus - 1, design, mates))

    @pl.when(locus < n_locus - 1)
    def _():
        greet((group, locus + 1, design, mates))

    bucket_row = owners_ref[...] - me
    bucket_row = jnp.where(bucket_row < 0, bucket_row + peers, bucket_row)
    member = (iota((peers, wins), 0) == bucket_row).astype(jnp.float32)
    before = (iota((wins, wins), 0) < iota((wins, wins), 1)).astype(jnp.bfloat16)
    earlier = dot(member.astype(jnp.bfloat16), before)
    rank_row = jnp.sum(earlier * member, axis=0, keepdims=True).astype(jnp.int32)
    place_row = bucket_row * cap + rank_row
    placer = (iota((peers * cap, wins), 0) == place_row).astype(jnp.bfloat16)
    picked = dot(placer, deltas_ref[:, own_columns]).astype(jnp.bfloat16)
    send_rows[...] = picked.reshape(peers, cap, half_width)
    lane_row = jnp.bitwise_and(place_row, 127)
    lanes = (iota((128, wins), 0) == lane_row).astype(jnp.bfloat16)
    slot_row = slots_ref[...].astype(jnp.float32)
    slot_table = dot_nt((member * slot_row).astype(jnp.bfloat16), lanes)
    for step in range(peers):
        send_slots[step] = jnp.broadcast_to(slot_table[step : step + 1, :], (8, 128))

    callers = peers + jnp.where(locus > 0, 1, 0) + jnp.where(locus < n_locus - 1, 1, 0)
    pl.semaphore_wait(barrier, callers)

    def remote(source, target, sems, index, device):
        return pltpu.make_async_remote_copy(
            src_ref=source,
            dst_ref=target,
            send_sem=sems.at[0, index],
            recv_sem=sems.at[1, index],
            device_id=device,
            device_id_type=MESH,
        )

    row_copies, slot_copies = [], []
    for step in range(1, peers):
        device = peer((me + step) % peers)
        slot_copies.append(
            remote(send_slots.at[step], recv_slots.at[step], slots_sem, step, device)
        )
        row_copies.append(remote(send_rows.at[step], recv_rows.at[step], rows_sem, step, device))
        slot_copies[-1].start()
        row_copies[-1].start()
    stem_copy = remote(stem_hbm, stem_ref.at[:, own_stem], stem_sem, 0, partner)
    stem_copy.start()

    recv_rows[0] = send_rows[0]
    recv_slots[0] = send_slots[0]
    place_column = to_column(place_row.astype(jnp.float32)).astype(jnp.int32)

    @pl.when(locus == 0)
    def _():
        seq_ref[0:2] = jnp.zeros((2,) + seq_ref.shape[1:], jnp.bfloat16)

    @pl.when(locus == n_locus - 1)
    def _():
        seq_ref[blocks + 2 : blocks + 4] = jnp.zeros((2,) + seq_ref.shape[1:], jnp.bfloat16)

    line = iota((64, 128), 0)
    wanted = (line // 16) * 32 + (line % 8) * 4 + core * 2 + (line // 8) % 2
    shuffle = (wanted == iota((64, 128), 1)).astype(jnp.bfloat16)
    base_own = jnp.concatenate(
        [dot(shuffle, base_ref[0, 128 * part : 128 * part + 128, :]) for part in range(blocks // 4)],
        axis=0,
    )
    load_mix.wait()
    head_row = head_ref[...]
    mix_grad = dot_nt(jnp.broadcast_to(head_row, (16, channels)), mix_ref[...])[0:1, :]

    for copy in slot_copies:
        copy.wait_recv()
    per = 128 // cap
    slot_rows = []
    for part in range(peers // per):
        total = recv_slots[part * per]
        for step in range(part * per + 1, part * per + per):
            total = total + recv_slots[step]
        slot_rows.append(total[0:1, :])
    gathers = [iota((slots, 128), 0) == row.astype(jnp.int32) for row in slot_rows]
    chooser = jnp.concatenate(
        [
            (to_column(row).astype(jnp.int32) == iota((128, slots), 1)).astype(jnp.bfloat16)
            for row in slot_rows
        ],
        axis=0,
    )
    for copy in row_copies:
        copy.wait_recv()
    edit = jnp.zeros((slots, half_width), jnp.float32)
    for part, gather in enumerate(gathers):
        rows = recv_rows[part * per : part * per + per].reshape(128, half_width)
        edit = edit + dot(gather.astype(jnp.bfloat16), rows)
    edit_own = jnp.stack(
        [edit[:, 0:128].reshape(blocks, 8, 128), edit[:, 128:256].reshape(blocks, 8, 128)], axis=1
    ).reshape(blocks * 16, 128)
    seq_own = (base_own + edit_own).astype(jnp.bfloat16)
    seq_ref[pl.ds(2, blocks), core] = seq_own.reshape(blocks, 16, 128)

    mine = seq_ref.at[pl.ds(2, blocks), core]
    seq_copy = remote(mine, mine, seq_sem, 0, partner)
    first, last = seq_ref.at[pl.ds(2, 2), core], seq_ref.at[pl.ds(blocks, 2), core]
    past, ahead = seq_ref.at[pl.ds(0, 2), core], seq_ref.at[pl.ds(blocks + 2, 2), core]
    up = [
        remote(last, past, halo_sem, 0, (group, locus + 1, design, core)),
        remote(last, past, halo_sem, 1, (group, locus + 1, design, mates)),
    ]
    down = [
        remote(first, ahead, halo_sem, 2, (group, locus - 1, design, core)),
        remote(first, ahead, halo_sem, 3, (group, locus - 1, design, mates)),
    ]

    @pl.when(locus < n_locus - 1)
    def _():
        for copy in up:
            copy.start()

    @pl.when(locus > 0)
    def _():
        for copy in down:
            copy.start()

    seq_copy.start()
    load_stem.wait()
    stem_copy.wait()
    load_taps.wait()
    seq_copy.wait()

    @pl.when(locus > 0)
    def _():
        for copy in up:
            copy.wait_recv()

    @pl.when(locus < n_locus - 1)
    def _():
        for copy in down:
            copy.wait_recv()

    rows_all = (blocks + 4) * 32
    conv_rows = (blocks + 2) * 32
    seq_all = seq_ref[...].reshape(rows_all, 128)
    for part in range(tiles):
        columns = slice(part * tile, part * tile + tile)
        pre_act = dot(seq_all, stem_ref[:, columns])
        hidden_ref[:, columns] = gelu_value(pre_act).astype(jnp.bfloat16)

    conv = dot(hidden_ref[0:conv_rows, :], taps_ref[0])
    for tap in range(1, 3):
        conv = conv + dot(hidden_ref[32 * tap : 32 * tap + conv_rows, :], taps_ref[tap])
    branch = (silu_slope(conv) * mix_grad).astype(jnp.bfloat16)
    branch_ref[...] = branch.reshape(branch_ref.shape)

    @pl.when(locus == 0)
    def _():
        branch_ref[0] = jnp.zeros(branch_ref.shape[1:], jnp.bfloat16)

    @pl.when(locus == n_locus - 1)
    def _():
        branch_ref[blocks + 1] = jnp.zeros(branch_ref.shape[1:], jnp.bfloat16)

    own_rows = blocks * 16

    def taps_of(side):
        return [
            branch_ref[pl.ds(2 - tap, blocks), side].reshape(own_rows, branch_ref.shape[3])
            for tap in range(3)
        ]

    def back_tile(inputs, part):
        lines = slice(part * tile, part * tile + tile)
        total = dot_nt(inputs[0], taps_ref[0, lines, :])
        for tap in range(1, 3):
            total = total + dot_nt(inputs[tap], taps_ref[tap, lines, :])
        return total

    theirs = taps_of(mates)
    part_copies = []
    for part in range(tiles):
        part_send[part] = back_tile(theirs, part).astype(jnp.bfloat16)
        part_copies.append(
            remote(part_send.at[part], part_recv.at[part], part_sem, part, partner)
        )
        part_copies[-1].start()
    ours = taps_of(core)
    seq_grad = jnp.zeros((own_rows, 128), jnp.float32)
    for part in range(tiles):
        columns = slice(part * tile, part * tile + tile)
        own = back_tile(ours, part) + head_row[:, columns].astype(jnp.float32)
        slope = gelu_slope(dot(seq_own, stem_ref[:, columns]))
        part_copies[part].wait_recv()
        pulled = slope * (own + part_recv[part].astype(jnp.float32))
        seq_grad = seq_grad + dot_nt(pulled.astype(jnp.bfloat16), stem_ref[:, columns])

    grads = seq_grad.reshape(blocks, 2, 8, 128)
    slot_grad = jnp.concatenate(
        [grads[:, 0].reshape(slots, 128), grads[:, 1].reshape(slots, 128)], axis=1
    ).astype(jnp.bfloat16)
    back = dot(chooser, slot_grad).astype(jnp.bfloat16)
    back_ref[...] = back.reshape(back_ref.shape)
    back_copies = []
    for step in range(1, peers):
        device = peer((me + peers - step) % peers)
        back_copies.append(remote(back_ref.at[step], ret_ref.at[step], back_sem, step, device))
        back_copies[-1].start()
    ret_ref[0] = back_ref[0]
    unplacer = (place_column == iota((wins, peers * cap), 1)).astype(jnp.bfloat16)
    for copy in back_copies:
        copy.wait_recv()
    result = dot(unplacer, ret_ref[...].reshape(peers * cap, half_width))
    half_ref[...] = result.astype(jnp.bfloat16)
    half_copy = remote(half_ref, other_ref, half_sem, 0, partner)
    half_copy.start()
    out_ref[:, own_columns] = result
    for copy in slot_copies + row_copies + part_copies + back_copies:
        copy.wait_send()

    @pl.when(locus < n_locus - 1)
    def _():
        for copy in up:
            copy.wait_send()

    @pl.when(locus > 0)
    def _():
        for copy in down:
            copy.wait_send()

    half_copy.wait()
    out_ref[:, other_columns] = other_ref[...].astype(jnp.float32)


def fused(
    n_locus,
    n_design,
    base_seq,
    deltas,
    owners,
    slot_ids,
    stem_weight,
    dilated_tap_weight,
    mix_weight,
    head_weight,
):
    wins, width = deltas.shape
    peers = n_locus * n_design
    cap = 2 * wins // peers
    blocks = base_seq.shape[1] // DILATION_STEP
    channels, own_width = dilated_tap_weight.shape[1:]
    feats = base_seq.shape[2]
    tile = 256
    tiles = channels // tile
    bf16, f32 = jnp.bfloat16, jnp.float32
    whole = pl.BlockSpec(memory_space=pltpu.VMEM)
    anywhere = pl.BlockSpec(memory_space=pl.ANY)
    pair = pltpu.SemaphoreType.DMA
    return pl.pallas_call(
        functools.partial(kernel, n_locus, n_design),
        out_shape=jax.ShapeDtypeStruct((wins, width), f32),
        in_specs=[whole, whole, whole, whole, anywhere, anywhere, anywhere, whole],
        out_specs=whole,
        scratch_shapes=[
            pltpu.VMEM((feats, channels), bf16),
            pltpu.VMEM(dilated_tap_weight.shape, bf16),
            pltpu.VMEM(mix_weight.shape, bf16),
            pltpu.VMEM((peers, cap, width // 2), bf16),
            pltpu.VMEM((peers, 8, 128), f32),
            pltpu.VMEM((peers, cap, width // 2), bf16),
            pltpu.VMEM((peers, 8, 128), f32),
            pltpu.VMEM((blocks + 4, 2, 16, feats), bf16),
            pltpu.VMEM(((blocks + 4) * 32, channels), bf16),
            pltpu.VMEM((blocks + 2, 2, 16, own_width), bf16),
            pltpu.VMEM((tiles, blocks * 16, tile), bf16),
            pltpu.VMEM((tiles, blocks * 16, tile), bf16),
            pltpu.VMEM((peers, cap, width // 2), bf16),
            pltpu.VMEM((peers, cap, width // 2), bf16),
            pltpu.VMEM((wins, width // 2), bf16),
            pltpu.VMEM((wins, width // 2), bf16),
            pair((3,)),
            pair((2, peers)),
            pair((2, peers)),
            pair((2, 1)),
            pair((2, 1)),
            pair((2, 4)),
            pair((2, tiles)),
            pair((2, peers)),
            pair((2, 1)),
        ],
        compiler_params=pltpu.CompilerParams(
            collective_id=0, has_side_effects=True, vmem_limit_bytes=60 * 1024 * 1024
        ),
    )(
        base_seq,
        deltas,
        owners.reshape(1, wins),
        slot_ids.reshape(1, wins),
        stem_weight,
        dilated_tap_weight,
        mix_weight,
        head_weight.reshape(1, channels),
    )


def body(n_locus, n_design, *arrays):
    base_seq, deltas = arrays[0], arrays[1]
    wins, width = deltas.shape
    peers = n_locus * n_design
    fits = (
        2 * wins == 32 * peers
        and wins == 128
        and width == 512
        and base_seq.shape[2] == 128
        and base_seq.shape[1] == 512
    )
    if fits:
        return fused(n_locus, n_design, *arrays)
    return shards(*arrays)


def solution(mesh):
    placed = (
        P(("groups", "design"), "locus", None),
        P(("groups", "locus", "design"), None),
        P(("groups", "locus", "design"), None),
        P(("groups", "locus", "design")),
        P(None, "chan"),
        P(None, None, "chan"),
        P("chan", None),
        P(),
    )
    return jax.shard_map(
        functools.partial(body, mesh.shape["locus"], mesh.shape["design"]),
        mesh=mesh,
        in_specs=placed,
        out_specs=P(("groups", "locus", "design"), None),
        check_vma=False,
    )
```

```python
import functools

import jax
import jax.numpy as jnp
from jax import lax
from jax.experimental import pallas as pl
from jax.experimental.pallas import tpu as pltpu
from jax.sharding import PartitionSpec as P

DILATION_STEP = 32
MESH = pl.DeviceIdType.MESH
NT = (((1,), (1,)), ((), ()))


def with_halo(cells, sides, width):
    for axis, dim in sides:
        count = lax.axis_size(axis)
        ends = count - 1
        head = lax.slice_in_dim(cells, 0, width, axis=dim)
        tail = lax.slice_in_dim(cells, cells.shape[dim] - width, cells.shape[dim], axis=dim)
        cells = jnp.concatenate(
            [
                lax.ppermute(tail, axis, [(i, (i + 1) % count) for i in range(ends)]),
                cells,
                lax.ppermute(head, axis, [((i + 1) % count, i) for i in range(ends)]),
            ],
            axis=dim,
        )
    return cells


def silu_slope(pre_value):
    sigmoid_value = jax.nn.sigmoid(pre_value)
    return sigmoid_value * (1.0 + pre_value * (1.0 - sigmoid_value))


def gelu_pull(pre_act, cotangent):
    return jax.vjp(lambda argument: jax.nn.gelu(argument, approximate=True), pre_act)[1](cotangent)[
        0
    ]


def stem_back(pulled, weight):
    upper = pulled.astype(jnp.bfloat16)
    lower = (pulled - upper.astype(jnp.float32)).astype(jnp.bfloat16)
    dims = (((1,), (1,)), ((), ()))
    first = lax.dot_general(upper, weight, dims, preferred_element_type=jnp.float32)
    return first + lax.dot_general(lower, weight, dims, preferred_element_type=jnp.float32)


def shards(
    base_seq, deltas, owners, slot_ids, stem_weight, dilated_tap_weight, mix_weight, head_weight
):
    win_dev, row_width = deltas.shape
    bins_per_device, feat_width = (base_seq.shape[1], base_seq.shape[2])
    slots_dev = bins_per_device * feat_width // row_width
    peer_count = lax.axis_size(("locus", "design"))
    capacity = max(2, 2 * win_dev // peer_count)
    bucket_rows = peer_count * capacity
    target_dev = owners[:, 0]
    member = (target_dev[:, None] == jnp.arange(peer_count, dtype=jnp.int32)[None, :]).astype(
        jnp.int32
    )
    order = jnp.arange(win_dev, dtype=jnp.int32)
    before = (order[None, :] < order[:, None]).astype(jnp.bfloat16)
    earlier = jnp.dot(
        before, member.astype(jnp.bfloat16), preferred_element_type=jnp.float32
    ).astype(jnp.int32)
    bucket_rank = jnp.sum(earlier * member, axis=1)
    position = target_dev * capacity + bucket_rank
    placer = position[None, :] == jnp.arange(bucket_rows, dtype=jnp.int32)[:, None]
    send_rows = jnp.dot(
        placer.astype(jnp.bfloat16), deltas, preferred_element_type=jnp.float32
    ).astype(jnp.bfloat16)
    send_slots = jnp.sum(jnp.where(placer, slot_ids[None, :], 0), axis=1)
    recv_rows, recv_slots = (
        lax.all_to_all(send_rows, ("locus", "design"), split_axis=0, concat_axis=0, tiled=True),
        lax.all_to_all(send_slots, ("locus", "design"), split_axis=0, concat_axis=0, tiled=True),
    )
    chooser = recv_slots[:, None] == jnp.arange(slots_dev, dtype=jnp.int32)[None, :]
    edit_sum = lax.dot_general(
        chooser.astype(jnp.bfloat16),
        recv_rows,
        (((0,), (0,)), ((), ())),
        preferred_element_type=jnp.float32,
    )
    sequence_onehot = (
        base_seq[0].astype(jnp.float32) + edit_sum.reshape(bins_per_device, feat_width)
    ).astype(jnp.bfloat16)
    padded_sequence = with_halo(sequence_onehot, (("locus", 0),), DILATION_STEP)
    stem_full = lax.all_gather(stem_weight, "chan", axis=1, tiled=True)
    gathered_preactivation = jnp.dot(padded_sequence, stem_full, preferred_element_type=jnp.float32)
    hidden_state = jax.nn.gelu(gathered_preactivation, approximate=True).astype(jnp.bfloat16)
    own_width = dilated_tap_weight.shape[2]
    convolved_output = jnp.zeros((bins_per_device, own_width), jnp.float32)
    for filter_tap in range(3):
        convolved_output = convolved_output + jnp.dot(
            hidden_state[filter_tap * DILATION_STEP : filter_tap * DILATION_STEP + bins_per_device],
            dilated_tap_weight[filter_tap],
            preferred_element_type=jnp.float32,
        )
    mix_grad = jnp.dot(mix_weight, head_weight, preferred_element_type=jnp.float32)
    residual_branch = (silu_slope(convolved_output) * mix_grad[None, :]).astype(jnp.bfloat16)
    padded_gradient = with_halo(residual_branch, (("locus", 0),), DILATION_STEP)
    part_sum = jnp.zeros((bins_per_device, stem_full.shape[1]), jnp.float32)
    for filter_tap in range(3):
        lower_boundary = (2 - filter_tap) * DILATION_STEP
        part_sum = part_sum + lax.dot_general(
            padded_gradient[lower_boundary : lower_boundary + bins_per_device],
            dilated_tap_weight[filter_tap],
            (((1,), (1,)), ((), ())),
            preferred_element_type=jnp.float32,
        )
    local_preactivation = gathered_preactivation[DILATION_STEP : DILATION_STEP + bins_per_device]
    summed = lax.psum(part_sum, "chan")
    hidden_grad = head_weight.astype(jnp.float32)[None, :] + summed
    pulled = gelu_pull(local_preactivation, hidden_grad)
    seq_grad = stem_back(pulled, stem_full)
    slot_grad = seq_grad.reshape(slots_dev, row_width)
    back_rows = jnp.dot(chooser.astype(jnp.float32), slot_grad, precision=lax.Precision.HIGHEST)
    returned = lax.all_to_all(
        back_rows, ("locus", "design"), split_axis=0, concat_axis=0, tiled=True
    )
    return lax.dot_general(
        placer.astype(jnp.float32),
        returned,
        (((0,), (0,)), ((), ())),
        precision=lax.Precision.HIGHEST,
    )


def dot(left, right):
    return jnp.dot(left, right, preferred_element_type=jnp.float32)


def dot_nt(left, right):
    return lax.dot_general(left, right, NT, preferred_element_type=jnp.float32)


def iota(shape, axis):
    return lax.broadcasted_iota(jnp.int32, shape, axis)


def to_column(row):
    count = row.shape[1]
    eye = iota((count, count), 0) == iota((count, count), 1)
    return jnp.sum(jnp.where(eye, row, 0.0), axis=1, keepdims=True)


def gelu_parts(value):
    square = value * value
    root = 0.7978845608028654
    curve = jnp.tanh(value * (root + (root * 0.044715) * square))
    return square, curve


def gelu_value(value):
    half = 0.5 * value
    return half + half * gelu_parts(value)[1]


def gelu_both(value):
    square, curve = gelu_parts(value)
    root = 0.7978845608028654
    inner = value * (root + (3.0 * root * 0.044715) * square)
    half = 0.5 * (1.0 + curve)
    return value * half, half + 0.5 * (1.0 - curve * curve) * inner


def kernel(
    n_locus,
    n_design,
    base_hbm,
    deltas_hbm,
    owners_ref,
    slots_ref,
    stem_hbm,
    taps_hbm,
    mix_hbm,
    head_ref,
    out_ref,
    base_ref,
    deltas_ref,
    stem_ref,
    taps_ref,
    mix_ref,
    send_rows,
    send_slots,
    recv_rows,
    recv_slots,
    seq_ref,
    hidden_ref,
    slope_ref,
    branch_ref,
    part_send,
    part_recv,
    back_ref,
    ret_ref,
    half_ref,
    other_ref,
    load_sem,
    rows_sem,
    slots_sem,
    stem_sem,
    seq_sem,
    halo_sem,
    part_sem,
    back_sem,
    half_sem,
):
    group, locus = lax.axis_index("groups"), lax.axis_index("locus")
    design, core = lax.axis_index("design"), lax.axis_index("chan")
    peers = n_locus * n_design
    me = locus * n_design + design
    wins, width = deltas_ref.shape
    half_width = width // 2
    cap = recv_rows.shape[1]
    stem_half = stem_hbm.shape[1]
    channels = stem_ref.shape[1]
    blocks = seq_ref.shape[0] - 4
    slots = blocks * 8
    tile = part_send.shape[2]
    tiles = channels // tile
    mates = 1 - core
    partner = (group, locus, design, mates)

    def peer(index):
        return (group, index // n_design, index % n_design, core)

    own_columns = pl.ds(pl.multiple_of(core * half_width, half_width), half_width)
    other_columns = pl.ds(pl.multiple_of(mates * half_width, half_width), half_width)
    own_stem = pl.ds(pl.multiple_of(core * stem_half, stem_half), stem_half)

    load_taps = pltpu.make_async_copy(taps_hbm, taps_ref, load_sem.at[0])
    load_mix = pltpu.make_async_copy(mix_hbm, mix_ref, load_sem.at[1])
    load_stem = pltpu.make_async_copy(stem_hbm, stem_ref.at[:, own_stem], load_sem.at[2])
    load_base = pltpu.make_async_copy(base_hbm, base_ref, load_sem.at[3])
    load_deltas = pltpu.make_async_copy(deltas_hbm, deltas_ref, load_sem.at[4])
    barrier = pltpu.get_barrier_semaphore()

    def greet(device):
        pl.semaphore_signal(barrier, inc=1, device_id=device, device_id_type=MESH)

    for step in range(1, peers):
        greet(peer((me + step) % peers))
    greet(partner)

    @pl.when(locus > 0)
    def _():
        greet((group, locus - 1, design, mates))

    @pl.when(locus < n_locus - 1)
    def _():
        greet((group, locus + 1, design, mates))

    load_deltas.start()
    load_base.start()
    load_stem.start()
    load_mix.start()
    load_taps.start()
    bucket_row = owners_ref[...] - me
    bucket_row = jnp.where(bucket_row < 0, bucket_row + peers, bucket_row)
    member = (iota((peers, wins), 0) == bucket_row).astype(jnp.float32)
    before = (iota((wins, wins), 0) < iota((wins, wins), 1)).astype(jnp.bfloat16)
    earlier = dot(member.astype(jnp.bfloat16), before)
    rank_row = jnp.sum(earlier * member, axis=0, keepdims=True).astype(jnp.int32)
    place_row = bucket_row * cap + rank_row
    placer = (iota((peers * cap, wins), 0) == place_row).astype(jnp.bfloat16)
    load_deltas.wait()
    picked = dot(placer, deltas_ref[:, own_columns]).astype(jnp.bfloat16)
    send_rows[...] = picked.reshape(peers, cap, half_width)
    lane_row = jnp.bitwise_and(place_row, 127)
    lanes = (iota((128, wins), 0) == lane_row).astype(jnp.bfloat16)
    slot_row = slots_ref[...].astype(jnp.float32)
    slot_table = dot_nt((member * slot_row).astype(jnp.bfloat16), lanes)
    for step in range(peers):
        send_slots[step] = jnp.broadcast_to(slot_table[step : step + 1, :], (8, 128))

    callers = peers + jnp.where(locus > 0, 1, 0) + jnp.where(locus < n_locus - 1, 1, 0)
    pl.semaphore_wait(barrier, callers)

    def remote(source, target, sems, index, device):
        return pltpu.make_async_remote_copy(
            src_ref=source,
            dst_ref=target,
            send_sem=sems.at[0, index],
            recv_sem=sems.at[1, index],
            device_id=device,
            device_id_type=MESH,
        )

    row_copies, slot_copies = [], []
    far_first = sorted(range(1, peers), key=lambda step: abs(2 * step - peers))
    for step in far_first:
        device = peer((me + step) % peers)
        slot_copies.append(
            remote(send_slots.at[step], recv_slots.at[step], slots_sem, step, device)
        )
        row_copies.append(remote(send_rows.at[step], recv_rows.at[step], rows_sem, step, device))
        slot_copies[-1].start()
        row_copies[-1].start()
    stem_copy = remote(stem_hbm, stem_ref.at[:, own_stem], stem_sem, 0, partner)
    stem_copy.start()

    recv_rows[0] = send_rows[0]
    recv_slots[0] = send_slots[0]
    place_column = to_column(place_row.astype(jnp.float32)).astype(jnp.int32)

    @pl.when(locus == 0)
    def _():
        seq_ref[0:2] = jnp.zeros((2,) + seq_ref.shape[1:], jnp.bfloat16)

    @pl.when(locus == n_locus - 1)
    def _():
        seq_ref[blocks + 2 : blocks + 4] = jnp.zeros((2,) + seq_ref.shape[1:], jnp.bfloat16)

    line = iota((64, 128), 0)
    wanted = (line // 16) * 32 + (line % 8) * 4 + core * 2 + (line // 8) % 2
    shuffle = (wanted == iota((64, 128), 1)).astype(jnp.bfloat16)
    load_base.wait()
    base_own = jnp.concatenate(
        [dot(shuffle, base_ref[0, 128 * part : 128 * part + 128, :]) for part in range(blocks // 4)],
        axis=0,
    )
    load_mix.wait()
    head_row = head_ref[...].astype(jnp.float32).reshape(1, channels)
    mix_grad = dot_nt(jnp.broadcast_to(head_row, (16, channels)).astype(jnp.bfloat16), mix_ref[...])[0:1, :]

    for copy in slot_copies:
        copy.wait_recv()
    per = 128 // cap
    slot_rows = []
    for part in range(peers // per):
        total = recv_slots[part * per]
        for step in range(part * per + 1, part * per + per):
            total = total + recv_slots[step]
        slot_rows.append(total[0:1, :])
    gathers = [iota((slots, 128), 0) == row.astype(jnp.int32) for row in slot_rows]
    chooser = jnp.concatenate(
        [
            (to_column(row).astype(jnp.int32) == iota((128, slots), 1)).astype(jnp.bfloat16)
            for row in slot_rows
        ],
        axis=0,
    )
    for copy in row_copies:
        copy.wait_recv()
    edit = jnp.zeros((slots, half_width), jnp.float32)
    for part, gather in enumerate(gathers):
        rows = recv_rows[part * per : part * per + per].reshape(128, half_width)
        edit = edit + dot(gather.astype(jnp.bfloat16), rows)
    edit_own = jnp.stack(
        [edit[:, 0:128].reshape(blocks, 8, 128), edit[:, 128:256].reshape(blocks, 8, 128)], axis=1
    ).reshape(blocks * 16, 128)
    seq_own = (base_own + edit_own).astype(jnp.bfloat16)
    seq_ref[pl.ds(2, blocks), core] = seq_own.reshape(blocks, 16, 128)

    mine = seq_ref.at[pl.ds(2, blocks), core]
    seq_copy = remote(mine, mine, seq_sem, 0, partner)
    first, last = seq_ref.at[pl.ds(2, 2), core], seq_ref.at[pl.ds(blocks, 2), core]
    past, ahead = seq_ref.at[pl.ds(0, 2), core], seq_ref.at[pl.ds(blocks + 2, 2), core]
    up = [
        remote(last, past, halo_sem, 0, (group, locus + 1, design, core)),
        remote(last, past, halo_sem, 1, (group, locus + 1, design, mates)),
    ]
    down = [
        remote(first, ahead, halo_sem, 2, (group, locus - 1, design, core)),
        remote(first, ahead, halo_sem, 3, (group, locus - 1, design, mates)),
    ]

    @pl.when(locus < n_locus - 1)
    def _():
        for copy in up:
            copy.start()

    @pl.when(locus > 0)
    def _():
        for copy in down:
            copy.start()

    seq_copy.start()
    load_stem.wait()
    stem_copy.wait()
    own_rows = blocks * 16
    for part in range(tiles):
        columns = slice(part * tile, part * tile + tile)
        pre_act = dot(seq_own, stem_ref[:, columns])
        value, slope_ref[:, columns] = gelu_both(pre_act)
        hidden_ref[pl.ds(2, blocks), core, :, columns] = value.astype(jnp.bfloat16).reshape(
            blocks, 16, tile
        )
    seq_copy.wait()
    seq_mate = seq_ref[pl.ds(2, blocks), mates].reshape(own_rows, 128)
    for part in range(tiles):
        columns = slice(part * tile, part * tile + tile)
        pre_act = dot(seq_mate, stem_ref[:, columns])
        hidden_ref[pl.ds(2, blocks), mates, :, columns] = (
            gelu_value(pre_act).astype(jnp.bfloat16).reshape(blocks, 16, tile)
        )

    @pl.when(locus > 0)
    def _():
        for copy in up:
            copy.wait_recv()

    @pl.when(locus < n_locus - 1)
    def _():
        for copy in down:
            copy.wait_recv()

    seq_edges = jnp.concatenate(
        [seq_ref[0:2].reshape(64, 128), seq_ref[blocks + 2 : blocks + 4].reshape(64, 128)], axis=0
    )
    for part in range(tiles):
        columns = slice(part * tile, part * tile + tile)
        value = gelu_value(dot(seq_edges, stem_ref[:, columns])).astype(jnp.bfloat16)
        value = value.reshape(4, 2, 16, tile)
        hidden_ref[0:2, :, :, columns] = value[0:2]
        hidden_ref[blocks + 2 : blocks + 4, :, :, columns] = value[2:4]

    conv_blocks = blocks + 2
    load_taps.wait()
    conv = jnp.zeros((conv_blocks * 32, taps_ref.shape[2]), jnp.float32)
    for tap in range(3):
        rows = hidden_ref[tap : tap + conv_blocks].reshape(conv_blocks * 32, channels)
        conv = conv + dot(rows, taps_ref[tap])
    branch = (silu_slope(conv) * mix_grad).astype(jnp.bfloat16)
    branch_ref[...] = branch.reshape(branch_ref.shape)

    @pl.when(locus == 0)
    def _():
        branch_ref[0] = jnp.zeros(branch_ref.shape[1:], jnp.bfloat16)

    @pl.when(locus == n_locus - 1)
    def _():
        branch_ref[blocks + 1] = jnp.zeros(branch_ref.shape[1:], jnp.bfloat16)

    def taps_of(side):
        return [
            branch_ref[pl.ds(2 - tap, blocks), side].reshape(own_rows, branch_ref.shape[3])
            for tap in range(3)
        ]

    def back_tile(inputs, part):
        lines = slice(part * tile, part * tile + tile)
        total = dot_nt(inputs[0], taps_ref[0, lines, :])
        for tap in range(1, 3):
            total = total + dot_nt(inputs[tap], taps_ref[tap, lines, :])
        return total

    theirs = taps_of(mates)
    part_copies = []
    for part in range(tiles):
        part_send[part] = back_tile(theirs, part).astype(jnp.bfloat16)
        part_copies.append(
            remote(part_send.at[part], part_recv.at[part], part_sem, part, partner)
        )
        part_copies[-1].start()
    ours = taps_of(core)
    seq_grad = jnp.zeros((own_rows, 128), jnp.float32)
    for part in range(tiles):
        columns = slice(part * tile, part * tile + tile)
        own = back_tile(ours, part) + head_row[:, columns]
        part_copies[part].wait_recv()
        pulled = slope_ref[:, columns] * (own + part_recv[part].astype(jnp.float32))
        seq_grad = seq_grad + dot_nt(pulled.astype(jnp.bfloat16), stem_ref[:, columns])

    grads = seq_grad.reshape(blocks, 2, 8, 128)
    slot_grad = jnp.concatenate(
        [grads[:, 0].reshape(slots, 128), grads[:, 1].reshape(slots, 128)], axis=1
    ).astype(jnp.bfloat16)
    back = dot(chooser, slot_grad).astype(jnp.bfloat16)
    back_ref[...] = back.reshape(back_ref.shape)
    back_copies = []
    for step in far_first:
        device = peer((me + peers - step) % peers)
        back_copies.append(remote(back_ref.at[step], ret_ref.at[step], back_sem, step, device))
        back_copies[-1].start()
    ret_ref[0] = back_ref[0]
    unplacer = (place_column == iota((wins, peers * cap), 1)).astype(jnp.bfloat16)
    for copy in back_copies:
        copy.wait_recv()
    result = dot(unplacer, ret_ref[...].reshape(peers * cap, half_width))
    result = result.astype(jnp.bfloat16)
    half_ref[...] = result
    half_copy = remote(half_ref, other_ref, half_sem, 0, partner)
    half_copy.start()
    out_ref[:, own_columns] = result
    for copy in slot_copies + row_copies + part_copies + back_copies:
        copy.wait_send()

    @pl.when(locus < n_locus - 1)
    def _():
        for copy in up:
            copy.wait_send()

    @pl.when(locus > 0)
    def _():
        for copy in down:
            copy.wait_send()

    half_copy.wait()
    out_ref[:, other_columns] = other_ref[...]


def fused(
    n_locus,
    n_design,
    base_seq,
    deltas,
    owners,
    slot_ids,
    stem_weight,
    dilated_tap_weight,
    mix_weight,
    head_weight,
):
    wins, width = deltas.shape
    peers = n_locus * n_design
    cap = 2 * wins // peers
    blocks = base_seq.shape[1] // DILATION_STEP
    channels, own_width = dilated_tap_weight.shape[1:]
    feats = base_seq.shape[2]
    tile = 256
    tiles = channels // tile
    bf16, f32 = jnp.bfloat16, jnp.float32
    whole = pl.BlockSpec(memory_space=pltpu.VMEM)
    anywhere = pl.BlockSpec(memory_space=pl.ANY)
    pair = pltpu.SemaphoreType.DMA
    return pl.pallas_call(
        functools.partial(kernel, n_locus, n_design),
        out_shape=jax.ShapeDtypeStruct((wins, width), bf16),
        in_specs=[anywhere, anywhere, whole, whole, anywhere, anywhere, anywhere, whole],
        out_specs=whole,
        scratch_shapes=[
            pltpu.VMEM(base_seq.shape, bf16),
            pltpu.VMEM(deltas.shape, bf16),
            pltpu.VMEM((feats, channels), bf16),
            pltpu.VMEM(dilated_tap_weight.shape, bf16),
            pltpu.VMEM(mix_weight.shape, bf16),
            pltpu.VMEM((peers, cap, width // 2), bf16),
            pltpu.VMEM((peers, 8, 128), f32),
            pltpu.VMEM((peers, cap, width // 2), bf16),
            pltpu.VMEM((peers, 8, 128), f32),
            pltpu.VMEM((blocks + 4, 2, 16, feats), bf16),
            pltpu.VMEM((blocks + 4, 2, 16, channels), bf16),
            pltpu.VMEM((blocks * 16, channels), f32),
            pltpu.VMEM((blocks + 2, 2, 16, own_width), bf16),
            pltpu.VMEM((tiles, blocks * 16, tile), bf16),
            pltpu.VMEM((tiles, blocks * 16, tile), bf16),
            pltpu.VMEM((peers, cap, width // 2), bf16),
            pltpu.VMEM((peers, cap, width // 2), bf16),
            pltpu.VMEM((wins, width // 2), bf16),
            pltpu.VMEM((wins, width // 2), bf16),
            pair((5,)),
            pair((2, peers)),
            pair((2, peers)),
            pair((2, 1)),
            pair((2, 1)),
            pair((2, 4)),
            pair((2, tiles)),
            pair((2, peers)),
            pair((2, 1)),
        ],
        compiler_params=pltpu.CompilerParams(
            collective_id=0, has_side_effects=True, vmem_limit_bytes=60 * 1024 * 1024
        ),
    )(
        base_seq,
        deltas,
        owners.reshape(1, wins),
        slot_ids.reshape(1, wins),
        stem_weight,
        dilated_tap_weight,
        mix_weight,
        head_weight,
    ).astype(f32)


def body(n_locus, n_design, *arrays):
    base_seq, deltas = arrays[0], arrays[1]
    wins, width = deltas.shape
    peers = n_locus * n_design
    fits = (
        2 * wins == 32 * peers
        and wins == 128
        and width == 512
        and base_seq.shape[2] == 128
        and base_seq.shape[1] == 512
    )
    if fits:
        return fused(n_locus, n_design, *arrays)
    return shards(*arrays)


def solution(mesh):
    placed = (
        P(("groups", "design"), "locus", None),
        P(("groups", "locus", "design"), None),
        P(("groups", "locus", "design"), None),
        P(("groups", "locus", "design")),
        P(None, "chan"),
        P(None, None, "chan"),
        P("chan", None),
        P(),
    )
    return jax.shard_map(
        functools.partial(body, mesh.shape["locus"], mesh.shape["design"]),
        mesh=mesh,
        in_specs=placed,
        out_specs=P(("groups", "locus", "design"), None),
        check_vma=False,
    )
```

```python
import functools

import jax
import jax.numpy as jnp
from jax import lax
from jax.experimental import pallas as pl
from jax.experimental.pallas import tpu as pltpu
from jax.sharding import PartitionSpec as P

DILATION_STEP = 32
MESH = pl.DeviceIdType.MESH
NT = (((1,), (1,)), ((), ()))


def with_halo(cells, sides, width):
    for axis, dim in sides:
        count = lax.axis_size(axis)
        ends = count - 1
        head = lax.slice_in_dim(cells, 0, width, axis=dim)
        tail = lax.slice_in_dim(cells, cells.shape[dim] - width, cells.shape[dim], axis=dim)
        cells = jnp.concatenate(
            [
                lax.ppermute(tail, axis, [(i, (i + 1) % count) for i in range(ends)]),
                cells,
                lax.ppermute(head, axis, [((i + 1) % count, i) for i in range(ends)]),
            ],
            axis=dim,
        )
    return cells


def silu_slope(pre_value):
    sigmoid_value = jax.nn.sigmoid(pre_value)
    return sigmoid_value * (1.0 + pre_value * (1.0 - sigmoid_value))


def gelu_pull(pre_act, cotangent):
    return jax.vjp(lambda argument: jax.nn.gelu(argument, approximate=True), pre_act)[1](cotangent)[
        0
    ]


def stem_back(pulled, weight):
    upper = pulled.astype(jnp.bfloat16)
    lower = (pulled - upper.astype(jnp.float32)).astype(jnp.bfloat16)
    dims = (((1,), (1,)), ((), ()))
    first = lax.dot_general(upper, weight, dims, preferred_element_type=jnp.float32)
    return first + lax.dot_general(lower, weight, dims, preferred_element_type=jnp.float32)


def shards(
    base_seq, deltas, owners, slot_ids, stem_weight, dilated_tap_weight, mix_weight, head_weight
):
    win_dev, row_width = deltas.shape
    bins_per_device, feat_width = (base_seq.shape[1], base_seq.shape[2])
    slots_dev = bins_per_device * feat_width // row_width
    peer_count = lax.axis_size(("locus", "design"))
    capacity = max(2, 2 * win_dev // peer_count)
    bucket_rows = peer_count * capacity
    target_dev = owners[:, 0]
    member = (target_dev[:, None] == jnp.arange(peer_count, dtype=jnp.int32)[None, :]).astype(
        jnp.int32
    )
    order = jnp.arange(win_dev, dtype=jnp.int32)
    before = (order[None, :] < order[:, None]).astype(jnp.bfloat16)
    earlier = jnp.dot(
        before, member.astype(jnp.bfloat16), preferred_element_type=jnp.float32
    ).astype(jnp.int32)
    bucket_rank = jnp.sum(earlier * member, axis=1)
    position = target_dev * capacity + bucket_rank
    placer = position[None, :] == jnp.arange(bucket_rows, dtype=jnp.int32)[:, None]
    send_rows = jnp.dot(
        placer.astype(jnp.bfloat16), deltas, preferred_element_type=jnp.float32
    ).astype(jnp.bfloat16)
    send_slots = jnp.sum(jnp.where(placer, slot_ids[None, :], 0), axis=1)
    recv_rows, recv_slots = (
        lax.all_to_all(send_rows, ("locus", "design"), split_axis=0, concat_axis=0, tiled=True),
        lax.all_to_all(send_slots, ("locus", "design"), split_axis=0, concat_axis=0, tiled=True),
    )
    chooser = recv_slots[:, None] == jnp.arange(slots_dev, dtype=jnp.int32)[None, :]
    edit_sum = lax.dot_general(
        chooser.astype(jnp.bfloat16),
        recv_rows,
        (((0,), (0,)), ((), ())),
        preferred_element_type=jnp.float32,
    )
    sequence_onehot = (
        base_seq[0].astype(jnp.float32) + edit_sum.reshape(bins_per_device, feat_width)
    ).astype(jnp.bfloat16)
    padded_sequence = with_halo(sequence_onehot, (("locus", 0),), DILATION_STEP)
    stem_full = lax.all_gather(stem_weight, "chan", axis=1, tiled=True)
    gathered_preactivation = jnp.dot(padded_sequence, stem_full, preferred_element_type=jnp.float32)
    hidden_state = jax.nn.gelu(gathered_preactivation, approximate=True).astype(jnp.bfloat16)
    own_width = dilated_tap_weight.shape[2]
    convolved_output = jnp.zeros((bins_per_device, own_width), jnp.float32)
    for filter_tap in range(3):
        convolved_output = convolved_output + jnp.dot(
            hidden_state[filter_tap * DILATION_STEP : filter_tap * DILATION_STEP + bins_per_device],
            dilated_tap_weight[filter_tap],
            preferred_element_type=jnp.float32,
        )
    mix_grad = jnp.dot(mix_weight, head_weight, preferred_element_type=jnp.float32)
    residual_branch = (silu_slope(convolved_output) * mix_grad[None, :]).astype(jnp.bfloat16)
    padded_gradient = with_halo(residual_branch, (("locus", 0),), DILATION_STEP)
    part_sum = jnp.zeros((bins_per_device, stem_full.shape[1]), jnp.float32)
    for filter_tap in range(3):
        lower_boundary = (2 - filter_tap) * DILATION_STEP
        part_sum = part_sum + lax.dot_general(
            padded_gradient[lower_boundary : lower_boundary + bins_per_device],
            dilated_tap_weight[filter_tap],
            (((1,), (1,)), ((), ())),
            preferred_element_type=jnp.float32,
        )
    local_preactivation = gathered_preactivation[DILATION_STEP : DILATION_STEP + bins_per_device]
    summed = lax.psum(part_sum, "chan")
    hidden_grad = head_weight.astype(jnp.float32)[None, :] + summed
    pulled = gelu_pull(local_preactivation, hidden_grad)
    seq_grad = stem_back(pulled, stem_full)
    slot_grad = seq_grad.reshape(slots_dev, row_width)
    back_rows = jnp.dot(chooser.astype(jnp.float32), slot_grad, precision=lax.Precision.HIGHEST)
    returned = lax.all_to_all(
        back_rows, ("locus", "design"), split_axis=0, concat_axis=0, tiled=True
    )
    return lax.dot_general(
        placer.astype(jnp.float32),
        returned,
        (((0,), (0,)), ((), ())),
        precision=lax.Precision.HIGHEST,
    )


def dot(left, right):
    return jnp.dot(left, right, preferred_element_type=jnp.float32)


def dot_nt(left, right):
    return lax.dot_general(left, right, NT, preferred_element_type=jnp.float32)


def iota(shape, axis):
    return lax.broadcasted_iota(jnp.int32, shape, axis)


def to_column(row):
    count = row.shape[1]
    eye = iota((count, count), 0) == iota((count, count), 1)
    return jnp.sum(jnp.where(eye, row, 0.0), axis=1, keepdims=True)


def gelu_parts(value):
    square = value * value
    root = 0.7978845608028654
    curve = jnp.tanh(value * (root + (root * 0.044715) * square))
    return square, curve


def gelu_value(value):
    half = 0.5 * value
    return half + half * gelu_parts(value)[1]


def gelu_both(value):
    square, curve = gelu_parts(value)
    root = 0.7978845608028654
    inner = value * (root + (3.0 * root * 0.044715) * square)
    half = 0.5 * (1.0 + curve)
    return value * half, half + 0.5 * (1.0 - curve * curve) * inner


def kernel(
    n_locus,
    n_design,
    base_hbm,
    deltas_hbm,
    owners_ref,
    slots_ref,
    stem_hbm,
    taps_hbm,
    mix_hbm,
    head_ref,
    out_ref,
    base_ref,
    deltas_ref,
    stem_ref,
    taps_ref,
    mix_ref,
    send_rows,
    send_slots,
    recv_rows,
    recv_slots,
    seq_ref,
    hidden_ref,
    slope_ref,
    branch_ref,
    part_send,
    part_recv,
    back_ref,
    ret_ref,
    half_ref,
    other_ref,
    load_sem,
    rows_sem,
    slots_sem,
    stem_sem,
    seq_sem,
    halo_sem,
    part_sem,
    back_sem,
    half_sem,
):
    group, locus = lax.axis_index("groups"), lax.axis_index("locus")
    design, core = lax.axis_index("design"), lax.axis_index("chan")
    peers = n_locus * n_design
    me = locus * n_design + design
    wins, width = deltas_ref.shape
    half_width = width // 2
    cap = recv_rows.shape[1]
    stem_half = stem_hbm.shape[1]
    channels = stem_ref.shape[1]
    blocks = seq_ref.shape[0] - 4
    slots = blocks * 8
    tile = part_send.shape[2]
    tiles = channels // tile
    mates = 1 - core
    partner = (group, locus, design, mates)

    def peer(index):
        return (group, index // n_design, index % n_design, core)

    own_columns = pl.ds(pl.multiple_of(core * half_width, half_width), half_width)
    other_columns = pl.ds(pl.multiple_of(mates * half_width, half_width), half_width)
    own_stem = pl.ds(pl.multiple_of(core * stem_half, stem_half), stem_half)

    load_taps = pltpu.make_async_copy(taps_hbm, taps_ref, load_sem.at[0])
    load_mix = pltpu.make_async_copy(mix_hbm, mix_ref, load_sem.at[1])
    load_stem = pltpu.make_async_copy(stem_hbm, stem_ref.at[:, own_stem], load_sem.at[2])
    load_base = pltpu.make_async_copy(base_hbm, base_ref, load_sem.at[3])
    load_deltas = pltpu.make_async_copy(deltas_hbm, deltas_ref, load_sem.at[4])
    barrier = pltpu.get_barrier_semaphore()

    def greet(device):
        pl.semaphore_signal(barrier, inc=1, device_id=device, device_id_type=MESH)

    for step in range(1, peers):
        greet(peer((me + step) % peers))
    greet(partner)

    @pl.when(locus > 0)
    def _():
        greet((group, locus - 1, design, mates))

    @pl.when(locus < n_locus - 1)
    def _():
        greet((group, locus + 1, design, mates))

    load_deltas.start()
    load_base.start()
    load_stem.start()
    load_mix.start()
    load_taps.start()
    bucket_row = owners_ref[...] - me
    bucket_row = jnp.where(bucket_row < 0, bucket_row + peers, bucket_row)
    member = (iota((peers, wins), 0) == bucket_row).astype(jnp.float32)
    before = (iota((wins, wins), 0) < iota((wins, wins), 1)).astype(jnp.bfloat16)
    earlier = dot(member.astype(jnp.bfloat16), before)
    rank_row = jnp.sum(earlier * member, axis=0, keepdims=True).astype(jnp.int32)
    place_row = bucket_row * cap + rank_row
    placer = (iota((peers * cap, wins), 0) == place_row).astype(jnp.bfloat16)
    load_deltas.wait()
    picked = dot(placer, deltas_ref[:, own_columns]).astype(jnp.bfloat16)
    send_rows[...] = picked.reshape(peers, cap, half_width)
    lane_row = jnp.bitwise_and(place_row, 127)
    lanes = (iota((128, wins), 0) == lane_row).astype(jnp.bfloat16)
    slot_row = slots_ref[...].astype(jnp.float32)
    slot_table = dot_nt((member * slot_row).astype(jnp.bfloat16), lanes)
    for step in range(peers):
        send_slots[step] = jnp.broadcast_to(slot_table[step : step + 1, :], (8, 128))

    callers = peers + jnp.where(locus > 0, 1, 0) + jnp.where(locus < n_locus - 1, 1, 0)
    pl.semaphore_wait(barrier, callers)

    def remote(source, target, sems, index, device):
        return pltpu.make_async_remote_copy(
            src_ref=source,
            dst_ref=target,
            send_sem=sems.at[0, index],
            recv_sem=sems.at[1, index],
            device_id=device,
            device_id_type=MESH,
        )

    row_copies, slot_copies = [], []
    far_first = sorted(range(1, peers), key=lambda step: abs(2 * step - peers))
    for step in far_first:
        device = peer((me + step) % peers)
        slot_copies.append(
            remote(send_slots.at[step], recv_slots.at[step], slots_sem, step, device)
        )
        row_copies.append(remote(send_rows.at[step], recv_rows.at[step], rows_sem, step, device))
        slot_copies[-1].start()
        row_copies[-1].start()
    stem_copy = remote(stem_hbm, stem_ref.at[:, own_stem], stem_sem, 0, partner)
    stem_copy.start()

    recv_rows[0] = send_rows[0]
    recv_slots[0] = send_slots[0]
    place_column = to_column(place_row.astype(jnp.float32)).astype(jnp.int32)

    @pl.when(locus == 0)
    def _():
        seq_ref[0:2] = jnp.zeros((2,) + seq_ref.shape[1:], jnp.bfloat16)

    @pl.when(locus == n_locus - 1)
    def _():
        seq_ref[blocks + 2 : blocks + 4] = jnp.zeros((2,) + seq_ref.shape[1:], jnp.bfloat16)

    line = iota((64, 128), 0)
    wanted = (line // 16) * 32 + (line % 8) * 4 + core * 2 + (line // 8) % 2
    shuffle = (wanted == iota((64, 128), 1)).astype(jnp.bfloat16)
    load_base.wait()
    base_own = jnp.concatenate(
        [dot(shuffle, base_ref[0, 128 * part : 128 * part + 128, :]) for part in range(blocks // 4)],
        axis=0,
    )
    load_mix.wait()
    head_row = head_ref[...].astype(jnp.float32).reshape(1, channels)
    mix_grad = dot_nt(jnp.broadcast_to(head_row, (16, channels)).astype(jnp.bfloat16), mix_ref[...])[0:1, :]

    for copy in slot_copies:
        copy.wait_recv()
    per = 128 // cap
    slot_rows = []
    for part in range(peers // per):
        total = recv_slots[part * per]
        for step in range(part * per + 1, part * per + per):
            total = total + recv_slots[step]
        slot_rows.append(total[0:1, :])
    gathers = [iota((slots, 128), 0) == row.astype(jnp.int32) for row in slot_rows]
    chooser = jnp.concatenate(
        [
            (to_column(row).astype(jnp.int32) == iota((128, slots), 1)).astype(jnp.bfloat16)
            for row in slot_rows
        ],
        axis=0,
    )
    for copy in row_copies:
        copy.wait_recv()
    edit = jnp.zeros((slots, half_width), jnp.float32)
    for part, gather in enumerate(gathers):
        rows = recv_rows[part * per : part * per + per].reshape(128, half_width)
        edit = edit + dot(gather.astype(jnp.bfloat16), rows)
    edit_own = jnp.stack(
        [edit[:, 0:128].reshape(blocks, 8, 128), edit[:, 128:256].reshape(blocks, 8, 128)], axis=1
    ).reshape(blocks * 16, 128)
    seq_own = (base_own + edit_own).astype(jnp.bfloat16)
    seq_ref[pl.ds(2, blocks), core] = seq_own.reshape(blocks, 16, 128)

    mine = seq_ref.at[pl.ds(2, blocks), core]
    seq_copy = remote(mine, mine, seq_sem, 0, partner)
    first, last = seq_ref.at[pl.ds(2, 2), core], seq_ref.at[pl.ds(blocks, 2), core]
    past, ahead = seq_ref.at[pl.ds(0, 2), core], seq_ref.at[pl.ds(blocks + 2, 2), core]
    up = [
        remote(last, past, halo_sem, 0, (group, locus + 1, design, core)),
        remote(last, past, halo_sem, 1, (group, locus + 1, design, mates)),
    ]
    down = [
        remote(first, ahead, halo_sem, 2, (group, locus - 1, design, core)),
        remote(first, ahead, halo_sem, 3, (group, locus - 1, design, mates)),
    ]

    @pl.when(locus < n_locus - 1)
    def _():
        for copy in up:
            copy.start()

    @pl.when(locus > 0)
    def _():
        for copy in down:
            copy.start()

    seq_copy.start()
    load_stem.wait()
    stem_copy.wait()
    own_rows = blocks * 16
    for part in range(tiles):
        columns = slice(part * tile, part * tile + tile)
        pre_act = dot(seq_own, stem_ref[:, columns])
        value, slope_ref[:, columns] = gelu_both(pre_act)
        hidden_ref[pl.ds(2, blocks), core, :, columns] = value.astype(jnp.bfloat16).reshape(
            blocks, 16, tile
        )
    seq_copy.wait()
    seq_mate = seq_ref[pl.ds(2, blocks), mates].reshape(own_rows, 128)
    for part in range(tiles):
        columns = slice(part * tile, part * tile + tile)
        pre_act = dot(seq_mate, stem_ref[:, columns])
        hidden_ref[pl.ds(2, blocks), mates, :, columns] = (
            gelu_value(pre_act).astype(jnp.bfloat16).reshape(blocks, 16, tile)
        )

    @pl.when(locus > 0)
    def _():
        for copy in up:
            copy.wait_recv()

    @pl.when(locus < n_locus - 1)
    def _():
        for copy in down:
            copy.wait_recv()

    seq_edges = jnp.concatenate(
        [seq_ref[0:2].reshape(64, 128), seq_ref[blocks + 2 : blocks + 4].reshape(64, 128)], axis=0
    )
    for part in range(tiles):
        columns = slice(part * tile, part * tile + tile)
        value = gelu_value(dot(seq_edges, stem_ref[:, columns])).astype(jnp.bfloat16)
        value = value.reshape(4, 2, 16, tile)
        hidden_ref[0:2, :, :, columns] = value[0:2]
        hidden_ref[blocks + 2 : blocks + 4, :, :, columns] = value[2:4]

    conv_blocks = blocks + 2
    load_taps.wait()

    def branch_of(side):
        conv = jnp.zeros((conv_blocks * 16, taps_ref.shape[2]), jnp.float32)
        for tap in range(3):
            rows = hidden_ref[tap : tap + conv_blocks, side].reshape(conv_blocks * 16, channels)
            conv = conv + dot(rows, taps_ref[tap])
        branch = (silu_slope(conv) * mix_grad).astype(jnp.bfloat16)
        branch_ref[:, side] = branch.reshape(conv_blocks, 16, taps_ref.shape[2])
        nothing = jnp.zeros((16, taps_ref.shape[2]), jnp.bfloat16)

        @pl.when(locus == 0)
        def _():
            branch_ref[0, side] = nothing

        @pl.when(locus == n_locus - 1)
        def _():
            branch_ref[blocks + 1, side] = nothing

    def taps_of(side):
        return [
            branch_ref[pl.ds(2 - tap, blocks), side].reshape(own_rows, branch_ref.shape[3])
            for tap in range(3)
        ]

    def back_tile(inputs, part):
        lines = slice(part * tile, part * tile + tile)
        total = dot_nt(inputs[0], taps_ref[0, lines, :])
        for tap in range(1, 3):
            total = total + dot_nt(inputs[tap], taps_ref[tap, lines, :])
        return total

    branch_of(mates)
    theirs = taps_of(mates)
    part_copies = []
    for part in range(tiles):
        part_send[part] = back_tile(theirs, part).astype(jnp.bfloat16)
        part_copies.append(
            remote(part_send.at[part], part_recv.at[part], part_sem, part, partner)
        )
        part_copies[-1].start()
    branch_of(core)
    ours = taps_of(core)
    seq_grad = jnp.zeros((own_rows, 128), jnp.float32)
    for part in range(tiles):
        columns = slice(part * tile, part * tile + tile)
        own = back_tile(ours, part) + head_row[:, columns]
        part_copies[part].wait_recv()
        pulled = slope_ref[:, columns] * (own + part_recv[part].astype(jnp.float32))
        seq_grad = seq_grad + dot_nt(pulled.astype(jnp.bfloat16), stem_ref[:, columns])

    grads = seq_grad.reshape(blocks, 2, 8, 128)
    slot_grad = jnp.concatenate(
        [grads[:, 0].reshape(slots, 128), grads[:, 1].reshape(slots, 128)], axis=1
    ).astype(jnp.bfloat16)
    back = dot(chooser, slot_grad).astype(jnp.bfloat16)
    back_ref[...] = back.reshape(back_ref.shape)
    back_copies = []
    for step in far_first:
        device = peer((me + peers - step) % peers)
        back_copies.append(remote(back_ref.at[step], ret_ref.at[step], back_sem, step, device))
        back_copies[-1].start()
    ret_ref[0] = back_ref[0]
    unplacer = (place_column == iota((wins, peers * cap), 1)).astype(jnp.bfloat16)
    for copy in back_copies:
        copy.wait_recv()
    result = dot(unplacer, ret_ref[...].reshape(peers * cap, half_width))
    result = result.astype(jnp.bfloat16)
    half_ref[...] = result
    half_copy = remote(half_ref, other_ref, half_sem, 0, partner)
    half_copy.start()
    out_ref[:, own_columns] = result
    for copy in slot_copies + row_copies + part_copies + back_copies:
        copy.wait_send()

    @pl.when(locus < n_locus - 1)
    def _():
        for copy in up:
            copy.wait_send()

    @pl.when(locus > 0)
    def _():
        for copy in down:
            copy.wait_send()

    half_copy.wait()
    out_ref[:, other_columns] = other_ref[...]


def fused(
    n_locus,
    n_design,
    base_seq,
    deltas,
    owners,
    slot_ids,
    stem_weight,
    dilated_tap_weight,
    mix_weight,
    head_weight,
):
    wins, width = deltas.shape
    peers = n_locus * n_design
    cap = 2 * wins // peers
    blocks = base_seq.shape[1] // DILATION_STEP
    channels, own_width = dilated_tap_weight.shape[1:]
    feats = base_seq.shape[2]
    tile = 256
    tiles = channels // tile
    bf16, f32 = jnp.bfloat16, jnp.float32
    whole = pl.BlockSpec(memory_space=pltpu.VMEM)
    anywhere = pl.BlockSpec(memory_space=pl.ANY)
    pair = pltpu.SemaphoreType.DMA
    return pl.pallas_call(
        functools.partial(kernel, n_locus, n_design),
        out_shape=jax.ShapeDtypeStruct((wins, width), bf16),
        in_specs=[anywhere, anywhere, whole, whole, anywhere, anywhere, anywhere, whole],
        out_specs=whole,
        scratch_shapes=[
            pltpu.VMEM(base_seq.shape, bf16),
            pltpu.VMEM(deltas.shape, bf16),
            pltpu.VMEM((feats, channels), bf16),
            pltpu.VMEM(dilated_tap_weight.shape, bf16),
            pltpu.VMEM(mix_weight.shape, bf16),
            pltpu.VMEM((peers, cap, width // 2), bf16),
            pltpu.VMEM((peers, 8, 128), f32),
            pltpu.VMEM((peers, cap, width // 2), bf16),
            pltpu.VMEM((peers, 8, 128), f32),
            pltpu.VMEM((blocks + 4, 2, 16, feats), bf16),
            pltpu.VMEM((blocks + 4, 2, 16, channels), bf16),
            pltpu.VMEM((blocks * 16, channels), f32),
            pltpu.VMEM((blocks + 2, 2, 16, own_width), bf16),
            pltpu.VMEM((tiles, blocks * 16, tile), bf16),
            pltpu.VMEM((tiles, blocks * 16, tile), bf16),
            pltpu.VMEM((peers, cap, width // 2), bf16),
            pltpu.VMEM((peers, cap, width // 2), bf16),
            pltpu.VMEM((wins, width // 2), bf16),
            pltpu.VMEM((wins, width // 2), bf16),
            pair((5,)),
            pair((2, peers)),
            pair((2, peers)),
            pair((2, 1)),
            pair((2, 1)),
            pair((2, 4)),
            pair((2, tiles)),
            pair((2, peers)),
            pair((2, 1)),
        ],
        compiler_params=pltpu.CompilerParams(
            collective_id=0, has_side_effects=True, vmem_limit_bytes=60 * 1024 * 1024
        ),
    )(
        base_seq,
        deltas,
        owners.reshape(1, wins),
        slot_ids.reshape(1, wins),
        stem_weight,
        dilated_tap_weight,
        mix_weight,
        head_weight,
    ).astype(f32)


def body(n_locus, n_design, *arrays):
    base_seq, deltas = arrays[0], arrays[1]
    wins, width = deltas.shape
    peers = n_locus * n_design
    fits = (
        2 * wins == 32 * peers
        and wins == 128
        and width == 512
        and base_seq.shape[2] == 128
        and base_seq.shape[1] == 512
    )
    if fits:
        return fused(n_locus, n_design, *arrays)
    return shards(*arrays)


def solution(mesh):
    placed = (
        P(("groups", "design"), "locus", None),
        P(("groups", "locus", "design"), None),
        P(("groups", "locus", "design"), None),
        P(("groups", "locus", "design")),
        P(None, "chan"),
        P(None, None, "chan"),
        P("chan", None),
        P(),
    )
    return jax.shard_map(
        functools.partial(body, mesh.shape["locus"], mesh.shape["design"]),
        mesh=mesh,
        in_specs=placed,
        out_specs=P(("groups", "locus", "design"), None),
        check_vma=False,
    )
```

```python
import functools

import jax
import jax.numpy as jnp
from jax import lax
from jax.experimental import pallas as pl
from jax.experimental.pallas import tpu as pltpu
from jax.sharding import PartitionSpec as P

DILATION_STEP = 32
MESH = pl.DeviceIdType.MESH
NT = (((1,), (1,)), ((), ()))


def with_halo(cells, sides, width):
    for axis, dim in sides:
        count = lax.axis_size(axis)
        ends = count - 1
        head = lax.slice_in_dim(cells, 0, width, axis=dim)
        tail = lax.slice_in_dim(cells, cells.shape[dim] - width, cells.shape[dim], axis=dim)
        cells = jnp.concatenate(
            [
                lax.ppermute(tail, axis, [(i, (i + 1) % count) for i in range(ends)]),
                cells,
                lax.ppermute(head, axis, [((i + 1) % count, i) for i in range(ends)]),
            ],
            axis=dim,
        )
    return cells


def silu_slope(pre_value):
    sigmoid_value = jax.nn.sigmoid(pre_value)
    return sigmoid_value * (1.0 + pre_value * (1.0 - sigmoid_value))


def gelu_pull(pre_act, cotangent):
    return jax.vjp(lambda argument: jax.nn.gelu(argument, approximate=True), pre_act)[1](cotangent)[
        0
    ]


def stem_back(pulled, weight):
    upper = pulled.astype(jnp.bfloat16)
    lower = (pulled - upper.astype(jnp.float32)).astype(jnp.bfloat16)
    dims = (((1,), (1,)), ((), ()))
    first = lax.dot_general(upper, weight, dims, preferred_element_type=jnp.float32)
    return first + lax.dot_general(lower, weight, dims, preferred_element_type=jnp.float32)


def shards(
    base_seq, deltas, owners, slot_ids, stem_weight, dilated_tap_weight, mix_weight, head_weight
):
    win_dev, row_width = deltas.shape
    bins_per_device, feat_width = (base_seq.shape[1], base_seq.shape[2])
    slots_dev = bins_per_device * feat_width // row_width
    peer_count = lax.axis_size(("locus", "design"))
    capacity = max(2, 2 * win_dev // peer_count)
    bucket_rows = peer_count * capacity
    target_dev = owners[:, 0]
    member = (target_dev[:, None] == jnp.arange(peer_count, dtype=jnp.int32)[None, :]).astype(
        jnp.int32
    )
    order = jnp.arange(win_dev, dtype=jnp.int32)
    before = (order[None, :] < order[:, None]).astype(jnp.bfloat16)
    earlier = jnp.dot(
        before, member.astype(jnp.bfloat16), preferred_element_type=jnp.float32
    ).astype(jnp.int32)
    bucket_rank = jnp.sum(earlier * member, axis=1)
    position = target_dev * capacity + bucket_rank
    placer = position[None, :] == jnp.arange(bucket_rows, dtype=jnp.int32)[:, None]
    send_rows = jnp.dot(
        placer.astype(jnp.bfloat16), deltas, preferred_element_type=jnp.float32
    ).astype(jnp.bfloat16)
    send_slots = jnp.sum(jnp.where(placer, slot_ids[None, :], 0), axis=1)
    recv_rows, recv_slots = (
        lax.all_to_all(send_rows, ("locus", "design"), split_axis=0, concat_axis=0, tiled=True),
        lax.all_to_all(send_slots, ("locus", "design"), split_axis=0, concat_axis=0, tiled=True),
    )
    chooser = recv_slots[:, None] == jnp.arange(slots_dev, dtype=jnp.int32)[None, :]
    edit_sum = lax.dot_general(
        chooser.astype(jnp.bfloat16),
        recv_rows,
        (((0,), (0,)), ((), ())),
        preferred_element_type=jnp.float32,
    )
    sequence_onehot = (
        base_seq[0].astype(jnp.float32) + edit_sum.reshape(bins_per_device, feat_width)
    ).astype(jnp.bfloat16)
    padded_sequence = with_halo(sequence_onehot, (("locus", 0),), DILATION_STEP)
    stem_full = lax.all_gather(stem_weight, "chan", axis=1, tiled=True)
    gathered_preactivation = jnp.dot(padded_sequence, stem_full, preferred_element_type=jnp.float32)
    hidden_state = jax.nn.gelu(gathered_preactivation, approximate=True).astype(jnp.bfloat16)
    own_width = dilated_tap_weight.shape[2]
    convolved_output = jnp.zeros((bins_per_device, own_width), jnp.float32)
    for filter_tap in range(3):
        convolved_output = convolved_output + jnp.dot(
            hidden_state[filter_tap * DILATION_STEP : filter_tap * DILATION_STEP + bins_per_device],
            dilated_tap_weight[filter_tap],
            preferred_element_type=jnp.float32,
        )
    mix_grad = jnp.dot(mix_weight, head_weight, preferred_element_type=jnp.float32)
    residual_branch = (silu_slope(convolved_output) * mix_grad[None, :]).astype(jnp.bfloat16)
    padded_gradient = with_halo(residual_branch, (("locus", 0),), DILATION_STEP)
    part_sum = jnp.zeros((bins_per_device, stem_full.shape[1]), jnp.float32)
    for filter_tap in range(3):
        lower_boundary = (2 - filter_tap) * DILATION_STEP
        part_sum = part_sum + lax.dot_general(
            padded_gradient[lower_boundary : lower_boundary + bins_per_device],
            dilated_tap_weight[filter_tap],
            (((1,), (1,)), ((), ())),
            preferred_element_type=jnp.float32,
        )
    local_preactivation = gathered_preactivation[DILATION_STEP : DILATION_STEP + bins_per_device]
    summed = lax.psum(part_sum, "chan")
    hidden_grad = head_weight.astype(jnp.float32)[None, :] + summed
    pulled = gelu_pull(local_preactivation, hidden_grad)
    seq_grad = stem_back(pulled, stem_full)
    slot_grad = seq_grad.reshape(slots_dev, row_width)
    back_rows = jnp.dot(chooser.astype(jnp.float32), slot_grad, precision=lax.Precision.HIGHEST)
    returned = lax.all_to_all(
        back_rows, ("locus", "design"), split_axis=0, concat_axis=0, tiled=True
    )
    return lax.dot_general(
        placer.astype(jnp.float32),
        returned,
        (((0,), (0,)), ((), ())),
        precision=lax.Precision.HIGHEST,
    )


def dot(left, right):
    return jnp.dot(left, right, preferred_element_type=jnp.float32)


def dot_nt(left, right):
    return lax.dot_general(left, right, NT, preferred_element_type=jnp.float32)


def iota(shape, axis):
    return lax.broadcasted_iota(jnp.int32, shape, axis)


def to_column(row):
    count = row.shape[1]
    eye = iota((count, count), 0) == iota((count, count), 1)
    return jnp.sum(jnp.where(eye, row, 0.0), axis=1, keepdims=True)


def gelu_parts(value):
    square = value * value
    root = 0.7978845608028654
    curve = jnp.tanh(value * (root + (root * 0.044715) * square))
    return square, curve


def gelu_value(value):
    half = 0.5 * value
    return half + half * gelu_parts(value)[1]


def gelu_both(value):
    square, curve = gelu_parts(value)
    root = 0.7978845608028654
    inner = value * (root + (3.0 * root * 0.044715) * square)
    half = 0.5 * (1.0 + curve)
    return value * half, half + 0.5 * (1.0 - curve * curve) * inner


def kernel(
    n_locus,
    n_design,
    base_hbm,
    deltas_hbm,
    owners_ref,
    slots_ref,
    stem_hbm,
    taps_hbm,
    mix_hbm,
    head_ref,
    out_ref,
    base_ref,
    deltas_ref,
    stem_ref,
    taps_ref,
    mix_ref,
    send_rows,
    send_slots,
    recv_rows,
    recv_slots,
    seq_ref,
    hidden_ref,
    slope_ref,
    branch_ref,
    part_send,
    part_recv,
    back_ref,
    ret_ref,
    half_ref,
    other_ref,
    load_sem,
    rows_sem,
    slots_sem,
    stem_sem,
    seq_sem,
    halo_sem,
    part_sem,
    back_sem,
    half_sem,
):
    group, locus = lax.axis_index("groups"), lax.axis_index("locus")
    design, core = lax.axis_index("design"), lax.axis_index("chan")
    peers = n_locus * n_design
    me = locus * n_design + design
    wins, width = deltas_ref.shape
    half_width = width // 2
    cap = recv_rows.shape[1]
    stem_half = stem_hbm.shape[1]
    channels = stem_ref.shape[1]
    blocks = seq_ref.shape[0] - 4
    slots = blocks * 8
    tile = part_send.shape[2]
    tiles = channels // tile
    mates = 1 - core
    partner = (group, locus, design, mates)

    def peer(index):
        return (group, index // n_design, index % n_design, core)

    own_columns = pl.ds(pl.multiple_of(core * half_width, half_width), half_width)
    other_columns = pl.ds(pl.multiple_of(mates * half_width, half_width), half_width)
    own_stem = pl.ds(pl.multiple_of(core * stem_half, stem_half), stem_half)

    load_taps = pltpu.make_async_copy(taps_hbm, taps_ref, load_sem.at[0])
    load_mix = pltpu.make_async_copy(mix_hbm, mix_ref, load_sem.at[1])
    load_stem = pltpu.make_async_copy(stem_hbm, stem_ref.at[:, own_stem], load_sem.at[2])
    load_base = pltpu.make_async_copy(base_hbm, base_ref, load_sem.at[3])
    load_deltas = pltpu.make_async_copy(deltas_hbm, deltas_ref, load_sem.at[4])
    barrier = pltpu.get_barrier_semaphore()

    def greet(device):
        pl.semaphore_signal(barrier, inc=1, device_id=device, device_id_type=MESH)

    for step in range(1, peers):
        greet(peer((me + step) % peers))
    greet(partner)

    @pl.when(locus > 0)
    def _():
        greet((group, locus - 1, design, mates))

    @pl.when(locus < n_locus - 1)
    def _():
        greet((group, locus + 1, design, mates))

    load_deltas.start()
    load_base.start()
    load_stem.start()
    load_mix.start()
    load_taps.start()
    bucket_row = owners_ref[...] - me
    bucket_row = jnp.where(bucket_row < 0, bucket_row + peers, bucket_row)
    member = (iota((peers, wins), 0) == bucket_row).astype(jnp.float32)
    before = (iota((wins, wins), 0) < iota((wins, wins), 1)).astype(jnp.bfloat16)
    earlier = dot(member.astype(jnp.bfloat16), before)
    rank_row = jnp.sum(earlier * member, axis=0, keepdims=True).astype(jnp.int32)
    place_row = bucket_row * cap + rank_row
    placer = (iota((peers * cap, wins), 0) == place_row).astype(jnp.bfloat16)
    load_deltas.wait()
    picked = dot(placer, deltas_ref[:, own_columns]).astype(jnp.bfloat16)
    send_rows[...] = picked.reshape(peers, cap, half_width)
    lane_row = jnp.bitwise_and(place_row, 127)
    lanes = (iota((128, wins), 0) == lane_row).astype(jnp.bfloat16)
    slot_row = slots_ref[...].astype(jnp.float32)
    slot_table = dot_nt((member * slot_row).astype(jnp.bfloat16), lanes)
    for step in range(peers):
        send_slots[step] = jnp.broadcast_to(slot_table[step : step + 1, :], (8, 128))

    callers = peers + jnp.where(locus > 0, 1, 0) + jnp.where(locus < n_locus - 1, 1, 0)
    pl.semaphore_wait(barrier, callers)

    def remote(source, target, sems, index, device):
        return pltpu.make_async_remote_copy(
            src_ref=source,
            dst_ref=target,
            send_sem=sems.at[0, index],
            recv_sem=sems.at[1, index],
            device_id=device,
            device_id_type=MESH,
        )

    row_copies, slot_copies = [], []
    far_first = sorted(range(1, peers), key=lambda step: abs(2 * step - peers))
    for step in far_first:
        device = peer((me + step) % peers)
        slot_copies.append(
            remote(send_slots.at[step], recv_slots.at[step], slots_sem, step, device)
        )
        row_copies.append(remote(send_rows.at[step], recv_rows.at[step], rows_sem, step, device))
        slot_copies[-1].start()
        row_copies[-1].start()
    stem_copy = remote(stem_hbm, stem_ref.at[:, own_stem], stem_sem, 0, partner)
    stem_copy.start()

    recv_rows[0] = send_rows[0]
    recv_slots[0] = send_slots[0]
    place_column = to_column(place_row.astype(jnp.float32)).astype(jnp.int32)

    @pl.when(locus == 0)
    def _():
        seq_ref[0:2] = jnp.zeros((2,) + seq_ref.shape[1:], jnp.bfloat16)

    @pl.when(locus == n_locus - 1)
    def _():
        seq_ref[blocks + 2 : blocks + 4] = jnp.zeros((2,) + seq_ref.shape[1:], jnp.bfloat16)

    line = iota((64, 128), 0)
    wanted = (line // 16) * 32 + (line % 8) * 4 + core * 2 + (line // 8) % 2
    shuffle = (wanted == iota((64, 128), 1)).astype(jnp.bfloat16)
    load_base.wait()
    base_own = jnp.concatenate(
        [dot(shuffle, base_ref[0, 128 * part : 128 * part + 128, :]) for part in range(blocks // 4)],
        axis=0,
    )
    load_mix.wait()
    head_row = head_ref[...].astype(jnp.float32).reshape(1, channels)
    mix_grad = dot_nt(jnp.broadcast_to(head_row, (16, channels)).astype(jnp.bfloat16), mix_ref[...])[0:1, :]

    for copy in slot_copies:
        copy.wait_recv()
    per = 128 // cap
    slot_rows = []
    for part in range(peers // per):
        total = recv_slots[part * per]
        for step in range(part * per + 1, part * per + per):
            total = total + recv_slots[step]
        slot_rows.append(total[0:1, :])
    gathers = [iota((slots, 128), 0) == row.astype(jnp.int32) for row in slot_rows]
    chooser = jnp.concatenate(
        [
            (to_column(row).astype(jnp.int32) == iota((128, slots), 1)).astype(jnp.bfloat16)
            for row in slot_rows
        ],
        axis=0,
    )
    for copy in row_copies:
        copy.wait_recv()
    edit = jnp.zeros((slots, half_width), jnp.float32)
    for part, gather in enumerate(gathers):
        rows = recv_rows[part * per : part * per + per].reshape(128, half_width)
        edit = edit + dot(gather.astype(jnp.bfloat16), rows)
    edit_own = jnp.stack(
        [edit[:, 0:128].reshape(blocks, 8, 128), edit[:, 128:256].reshape(blocks, 8, 128)], axis=1
    ).reshape(blocks * 16, 128)
    seq_own = (base_own + edit_own).astype(jnp.bfloat16)
    seq_ref[pl.ds(2, blocks), core] = seq_own.reshape(blocks, 16, 128)

    mine = seq_ref.at[pl.ds(2, blocks), core]
    seq_copy = remote(mine, mine, seq_sem, 0, partner)
    first, last = seq_ref.at[pl.ds(2, 2), core], seq_ref.at[pl.ds(blocks, 2), core]
    past, ahead = seq_ref.at[pl.ds(0, 2), core], seq_ref.at[pl.ds(blocks + 2, 2), core]
    up = [
        remote(last, past, halo_sem, 0, (group, locus + 1, design, core)),
        remote(last, past, halo_sem, 1, (group, locus + 1, design, mates)),
    ]
    down = [
        remote(first, ahead, halo_sem, 2, (group, locus - 1, design, core)),
        remote(first, ahead, halo_sem, 3, (group, locus - 1, design, mates)),
    ]

    @pl.when(locus < n_locus - 1)
    def _():
        for copy in up:
            copy.start()

    @pl.when(locus > 0)
    def _():
        for copy in down:
            copy.start()

    seq_copy.start()
    load_stem.wait()
    stem_copy.wait()
    own_rows = blocks * 16
    for part in range(tiles):
        columns = slice(part * tile, part * tile + tile)
        pre_act = dot(seq_own, stem_ref[:, columns])
        value, slope_ref[:, columns] = gelu_both(pre_act)
        hidden_ref[pl.ds(2, blocks), core, :, columns] = value.astype(jnp.bfloat16).reshape(
            blocks, 16, tile
        )
    seq_copy.wait()
    seq_mate = seq_ref[pl.ds(2, blocks), mates].reshape(own_rows, 128)
    for part in range(tiles):
        columns = slice(part * tile, part * tile + tile)
        pre_act = dot(seq_mate, stem_ref[:, columns])
        hidden_ref[pl.ds(2, blocks), mates, :, columns] = (
            gelu_value(pre_act).astype(jnp.bfloat16).reshape(blocks, 16, tile)
        )

    @pl.when(locus > 0)
    def _():
        for copy in up:
            copy.wait_recv()

    @pl.when(locus < n_locus - 1)
    def _():
        for copy in down:
            copy.wait_recv()

    seq_edges = jnp.concatenate(
        [seq_ref[0:2].reshape(64, 128), seq_ref[blocks + 2 : blocks + 4].reshape(64, 128)], axis=0
    )
    for part in range(tiles):
        columns = slice(part * tile, part * tile + tile)
        value = gelu_value(dot(seq_edges, stem_ref[:, columns])).astype(jnp.bfloat16)
        value = value.reshape(4, 2, 16, tile)
        hidden_ref[0:2, :, :, columns] = value[0:2]
        hidden_ref[blocks + 2 : blocks + 4, :, :, columns] = value[2:4]

    conv_blocks = blocks + 2
    load_taps.wait()
    conv = jnp.zeros((conv_blocks * 32, taps_ref.shape[2]), jnp.float32)
    for tap in range(3):
        rows = hidden_ref[tap : tap + conv_blocks].reshape(conv_blocks * 32, channels)
        conv = conv + dot(rows, taps_ref[tap])
    branch = (silu_slope(conv) * mix_grad).astype(jnp.bfloat16)
    branch_ref[...] = branch.reshape(branch_ref.shape)

    @pl.when(locus == 0)
    def _():
        branch_ref[0] = jnp.zeros(branch_ref.shape[1:], jnp.bfloat16)

    @pl.when(locus == n_locus - 1)
    def _():
        branch_ref[blocks + 1] = jnp.zeros(branch_ref.shape[1:], jnp.bfloat16)

    def taps_of(side):
        return [
            branch_ref[pl.ds(2 - tap, blocks), side].reshape(own_rows, branch_ref.shape[3])
            for tap in range(3)
        ]

    def back_tile(inputs, part):
        lines = slice(part * tile, part * tile + tile)
        total = dot_nt(inputs[0], taps_ref[0, lines, :])
        for tap in range(1, 3):
            total = total + dot_nt(inputs[tap], taps_ref[tap, lines, :])
        return total

    both = [jnp.concatenate(pair, axis=0) for pair in zip(taps_of(mates), taps_of(core))]
    part_copies, kept = [], []
    seq_grad = jnp.zeros((own_rows, 128), jnp.float32)
    lag = 3
    for part in range(tiles + lag):
        if part < tiles:
            terms = back_tile(both, part)
            part_send[part] = terms[0:own_rows].astype(jnp.bfloat16)
            part_copies.append(
                remote(part_send.at[part], part_recv.at[part], part_sem, part, partner)
            )
            part_copies[-1].start()
            kept.append(terms[own_rows:])
        if part >= lag:
            done = part - lag
            columns = slice(done * tile, done * tile + tile)
            own = kept[done] + head_row[:, columns]
            part_copies[done].wait_recv()
            pulled = slope_ref[:, columns] * (own + part_recv[done].astype(jnp.float32))
            seq_grad = seq_grad + dot_nt(pulled.astype(jnp.bfloat16), stem_ref[:, columns])

    grads = seq_grad.reshape(blocks, 2, 8, 128)
    slot_grad = jnp.concatenate(
        [grads[:, 0].reshape(slots, 128), grads[:, 1].reshape(slots, 128)], axis=1
    ).astype(jnp.bfloat16)
    back = dot(chooser, slot_grad).astype(jnp.bfloat16)
    back_ref[...] = back.reshape(back_ref.shape)
    back_copies = []
    for step in far_first:
        device = peer((me + peers - step) % peers)
        back_copies.append(remote(back_ref.at[step], ret_ref.at[step], back_sem, step, device))
        back_copies[-1].start()
    ret_ref[0] = back_ref[0]
    unplacer = (place_column == iota((wins, peers * cap), 1)).astype(jnp.bfloat16)
    for copy in back_copies:
        copy.wait_recv()
    result = dot(unplacer, ret_ref[...].reshape(peers * cap, half_width))
    result = result.astype(jnp.bfloat16)
    half_ref[...] = result
    half_copy = remote(half_ref, other_ref, half_sem, 0, partner)
    half_copy.start()
    out_ref[:, own_columns] = result
    for copy in slot_copies + row_copies + part_copies + back_copies:
        copy.wait_send()

    @pl.when(locus < n_locus - 1)
    def _():
        for copy in up:
            copy.wait_send()

    @pl.when(locus > 0)
    def _():
        for copy in down:
            copy.wait_send()

    half_copy.wait()
    out_ref[:, other_columns] = other_ref[...]


def fused(
    n_locus,
    n_design,
    base_seq,
    deltas,
    owners,
    slot_ids,
    stem_weight,
    dilated_tap_weight,
    mix_weight,
    head_weight,
):
    wins, width = deltas.shape
    peers = n_locus * n_design
    cap = 2 * wins // peers
    blocks = base_seq.shape[1] // DILATION_STEP
    channels, own_width = dilated_tap_weight.shape[1:]
    feats = base_seq.shape[2]
    tile = 256
    tiles = channels // tile
    bf16, f32 = jnp.bfloat16, jnp.float32
    whole = pl.BlockSpec(memory_space=pltpu.VMEM)
    anywhere = pl.BlockSpec(memory_space=pl.ANY)
    pair = pltpu.SemaphoreType.DMA
    return pl.pallas_call(
        functools.partial(kernel, n_locus, n_design),
        out_shape=jax.ShapeDtypeStruct((wins, width), bf16),
        in_specs=[anywhere, anywhere, whole, whole, anywhere, anywhere, anywhere, whole],
        out_specs=whole,
        scratch_shapes=[
            pltpu.VMEM(base_seq.shape, bf16),
            pltpu.VMEM(deltas.shape, bf16),
            pltpu.VMEM((feats, channels), bf16),
            pltpu.VMEM(dilated_tap_weight.shape, bf16),
            pltpu.VMEM(mix_weight.shape, bf16),
            pltpu.VMEM((peers, cap, width // 2), bf16),
            pltpu.VMEM((peers, 8, 128), f32),
            pltpu.VMEM((peers, cap, width // 2), bf16),
            pltpu.VMEM((peers, 8, 128), f32),
            pltpu.VMEM((blocks + 4, 2, 16, feats), bf16),
            pltpu.VMEM((blocks + 4, 2, 16, channels), bf16),
            pltpu.VMEM((blocks * 16, channels), f32),
            pltpu.VMEM((blocks + 2, 2, 16, own_width), bf16),
            pltpu.VMEM((tiles, blocks * 16, tile), bf16),
            pltpu.VMEM((tiles, blocks * 16, tile), bf16),
            pltpu.VMEM((peers, cap, width // 2), bf16),
            pltpu.VMEM((peers, cap, width // 2), bf16),
            pltpu.VMEM((wins, width // 2), bf16),
            pltpu.VMEM((wins, width // 2), bf16),
            pair((5,)),
            pair((2, peers)),
            pair((2, peers)),
            pair((2, 1)),
            pair((2, 1)),
            pair((2, 4)),
            pair((2, tiles)),
            pair((2, peers)),
            pair((2, 1)),
        ],
        compiler_params=pltpu.CompilerParams(
            collective_id=0, has_side_effects=True, vmem_limit_bytes=60 * 1024 * 1024
        ),
    )(
        base_seq,
        deltas,
        owners.reshape(1, wins),
        slot_ids.reshape(1, wins),
        stem_weight,
        dilated_tap_weight,
        mix_weight,
        head_weight,
    ).astype(f32)


def body(n_locus, n_design, *arrays):
    base_seq, deltas = arrays[0], arrays[1]
    wins, width = deltas.shape
    peers = n_locus * n_design
    fits = (
        2 * wins == 32 * peers
        and wins == 128
        and width == 512
        and base_seq.shape[2] == 128
        and base_seq.shape[1] == 512
    )
    if fits:
        return fused(n_locus, n_design, *arrays)
    return shards(*arrays)


def solution(mesh):
    placed = (
        P(("groups", "design"), "locus", None),
        P(("groups", "locus", "design"), None),
        P(("groups", "locus", "design"), None),
        P(("groups", "locus", "design")),
        P(None, "chan"),
        P(None, None, "chan"),
        P("chan", None),
        P(),
    )
    return jax.shard_map(
        functools.partial(body, mesh.shape["locus"], mesh.shape["design"]),
        mesh=mesh,
        in_specs=placed,
        out_specs=P(("groups", "locus", "design"), None),
        check_vma=False,
    )
```
